128 devices in a mesh: dp: 16 (over z, x), tp: 8 (over y, core).
Axes of the slice: x: 4, y: 4, z: 4, core: 2. Of those that a mesh axis runs over, the one named last changes fastest.
Arguments:
- attn_out: bfloat16 [16384, 4096], P('dp', 'tp'), may hold values from -6 to 6
- residual_in: bfloat16 [16384, 5120], P('dp', 'tp'), may hold values from -6 to 6
- teacher: bfloat16 [16384, 5120], P('dp', 'tp'), may hold values from -6 to 6
- out_weight: bfloat16 [4096, 5120], P(None, 'tp'), may hold values from -0.09375 to 0.09375
- error_buf: bfloat16 [16, 4096, 5120], P('dp', None, 'tp'), may hold values from -6 to 6
- q_start: float32 [5120, 64], P('tp'), may hold values from -6 to 6
Outputs:
- error_next: bfloat16 [16, 4096, 5120], P('dp', None, 'tp')
- q_next: float32 [5120, 64], P('tp')
The draws below stay inside these ranges and needn't reach their ends.
All inputs are finite; a program needn't handle non-finite values.
Results may differ from the reference program's by a relative error of at most 0.015.
Values may be sent and summed in bfloat16 or wider, within the bound.
A program may use at most 128 MiB of HBM per device.

```python
import jax
import jax.numpy as jnp
from jax import lax

D = 5120
RANK = 64
TOK_DEV = 1024
ROWS = 4096
TOKENS = 16384
N_DP = 16


def levels(stream_key, shape, pieces, low, top_value):
    loudness, own = 1.0, jax.random.fold_in(stream_key, 6)
    for position, shards_of in pieces:
        steps = jnp.exp(jax.random.uniform(jax.random.fold_in(own, position), (shards_of,), jnp.float32, low / len(pieces), top_value / len(pieces)))
        loudness = loudness * jnp.repeat(steps, shape[position] // shards_of).reshape([-1 if axis == position else 1 for axis in range(len(shape))])
    return loudness


def normal_values(stream_key, dims, spread, limit, cuts=(), dtype=jnp.bfloat16):
    loudness = levels(stream_key, dims, cuts, -0.22, 0.18) if cuts else 1.0
    values = jax.random.normal(stream_key, dims, jnp.float32) * spread * loudness
    return jnp.minimum(jnp.maximum(values, -limit), limit).astype(dtype)


def setup_inputs(seed: int = 0) -> dict:
    keys = jax.random.split(jax.random.key(seed), 7)
    attn_out = normal_values(keys[0], (TOKENS, ROWS), 1.0, 6.0, ((0, 16), (1, 8)))
    residual_in = normal_values(keys[1], (TOKENS, D), 1.0, 6.0, ((0, 16), (1, 8)))
    teacher = normal_values(keys[2], (TOKENS, D), 1.0, 6.0, ((0, 16), (1, 8)))
    out_weight = normal_values(keys[3], (ROWS, D), ROWS ** -0.5, 0.09375, ((1, 8),))
    error_buf = normal_values(keys[4], (N_DP, ROWS, D), 1.0, 6.0, ((0, 16), (2, 8)))
    q_start = normal_values(keys[5], (D, RANK), 1.0, 6.0, ((0, 8),), jnp.float32)
    return {"attn_out": attn_out, "residual_in": residual_in, "teacher": teacher, "out_weight": out_weight, "error_buf": error_buf, "q_start": q_start}


def replica_matrix(inputs):
    heads_rep, resid_rep, teach_rep, error_rep, out_weight = inputs
    projected = jnp.dot(heads_rep.astype(jnp.float32), out_weight.astype(jnp.float32), preferred_element_type=jnp.float32)
    diff = (resid_rep.astype(jnp.float32) + projected - teach_rep.astype(jnp.float32)).astype(jnp.bfloat16)
    grad = jnp.dot(heads_rep.T.astype(jnp.float32), diff.astype(jnp.float32), preferred_element_type=jnp.float32)
    return grad * (1.0 / jnp.sqrt(jnp.float32(TOK_DEV))) + error_rep.astype(jnp.float32)

def orthonormal(factor):
    gram_matrix = jnp.dot(factor.T, factor, precision=lax.Precision.HIGHEST)
    lower_factor = jnp.linalg.cholesky(gram_matrix)
    return lax.linalg.triangular_solve(lower_factor, factor, left_side=False, lower=True, transpose_a=True)

def reference(attn_out, residual_in, teacher, out_weight, error_buf, q_start):
    heads_all = attn_out.reshape(N_DP, TOK_DEV, ROWS)
    resid_all = residual_in.reshape(N_DP, TOK_DEV, D)
    teach_all = teacher.reshape(N_DP, TOK_DEV, D)

    def one_replica(index):
        return replica_matrix((heads_all[index], resid_all[index], teach_all[index], error_buf[index], out_weight))
    matrices = lax.map(one_replica, jnp.arange(N_DP))
    left_sum = jnp.einsum('rij,jk->ik', matrices, q_start, precision=lax.Precision.HIGHEST) / N_DP
    basis = orthonormal(left_sum)
    q_next = jnp.einsum('rij,ik->jk', matrices, basis, precision=lax.Precision.HIGHEST) / N_DP
    approx = jnp.dot(basis, q_next.T, precision=lax.Precision.HIGHEST)
    error_next = (matrices - approx[None]).astype(jnp.bfloat16)
    return (error_next, q_next)
```

```python
import jax
import jax.numpy as jnp
from jax import lax
from jax.experimental import pallas as pl
from jax.experimental.pallas import tpu as pltpu
from jax.sharding import PartitionSpec as P

MESH = pl.DeviceIdType.MESH
F32, BF16 = jnp.float32, jnp.bfloat16
DP, TP = 16, 8
TOK, FEAT, COLS, RANK = 1024, 512, 640, 64
ROWS = FEAT * TP
PIECE = FEAT // DP
TOKP = TOK // TP
HALF = TOK // 2
CUTS = 2
CUT = HALF // CUTS
TILES = 48


def dot(a, b):
    return jnp.dot(a, b, preferred_element_type=F32)


def fold(x):
    return x + pltpu.roll(x, RANK, 1)


def split(x):
    lane = lax.broadcasted_iota(jnp.int32, x.shape, 1)
    high = x.astype(BF16).astype(F32)
    return jnp.where(lane < RANK, high, x - high).astype(BF16)


def split_rows(x):
    high = x.astype(BF16).astype(F32)
    low = x - high
    return (
        jnp.concatenate([high, high], axis=0).astype(BF16),
        jnp.concatenate([low, low], axis=0).astype(BF16),
    )


def inverse_factor(gram):
    lane = lax.broadcasted_iota(jnp.int32, (8, 128), 1)
    sub = lax.broadcasted_iota(jnp.int32, (8, 128), 0)
    blocks = []
    for b in range(8):
        eye = jnp.where(lane == sub + (RANK + 8 * b), 1.0, 0.0)
        blocks.append(jnp.where(lane < RANK, gram[8 * b : 8 * b + 8, :], eye))
    for k in range(RANK):
        home, at = k // 8, k % 8
        pivot = jnp.broadcast_to(blocks[home][at : at + 1, :], (8, 128))
        scaled = pivot / jnp.broadcast_to(pivot[:, k : k + 1], (8, 128))
        for b in range(home, 8):
            column = jnp.broadcast_to(blocks[b][:, k : k + 1], (8, 128))
            if b == home:
                column = jnp.where(sub > at, column, 0.0)
            blocks[b] = blocks[b] - column * scaled
    out = []
    for b in range(8):
        diagonal = jnp.sum(jnp.where(lane == sub + 8 * b, blocks[b], 0.0), axis=1, keepdims=True)
        rows = jnp.where(lane < RANK, 0.0, blocks[b] * lax.rsqrt(diagonal))
        out.append(fold(rows))
    return jnp.concatenate(out, axis=0)


def main_kernel(
    a_hbm, res_hbm, tch_hbm, w_hbm, e_hbm, qt_ref,
    m_hbm, phat_ref, qnext_ref,
    abuf, at, wv, ev, res, tch, proj, wblk, qcat, xq,
    wq_send, wq_recv, wq_full, dq_send, dq_recv, dq_full,
    pa_send, pa_recv, eq_send, e_recv, e2_send, e2_recv, pfull, pt,
    r_send, r_recv, r_full,
    load_sem, ag_send, ag_recv, x_send, x_recv, out_sem,
):
    d, t = lax.axis_index("dp"), lax.axis_index("tp")
    y, c = t // 2, lax.rem(t, 2)
    sib = y * 2 + 1 - c
    up = lax.rem(y + 1, 4) * 2 + c
    down = lax.rem(y + 3, 4) * 2 + c
    far = lax.rem(y + 2, 4) * 2 + c

    def other(owner):
        return (owner // 2) * 2 + 1 - lax.rem(owner, 2)

    load_blk = pltpu.make_async_copy(w_hbm.at[:, pl.ds(pl.multiple_of(d * PIECE, PIECE), PIECE)], wblk, load_sem.at[0])
    load_a = pltpu.make_async_copy(a_hbm, abuf.at[t], load_sem.at[1])
    load_e = pltpu.make_async_copy(e_hbm, ev, load_sem.at[2])
    load_res = pltpu.make_async_copy(res_hbm, res, load_sem.at[3])
    load_tch = pltpu.make_async_copy(tch_hbm, tch, load_sem.at[4])
    load_w = pltpu.make_async_copy(w_hbm, wv, load_sem.at[5])
    for load in (load_blk, load_a, load_e, load_res, load_tch, load_w):
        load.start()

    barrier = pltpu.get_barrier_semaphore()

    @pl.loop(1, TP)
    def _(k):
        pl.semaphore_signal(barrier, inc=1, device_id={"tp": lax.rem(t + k, TP)}, device_id_type=MESH)

    @pl.loop(1, DP)
    def _(k):
        pl.semaphore_signal(barrier, inc=1, device_id={"dp": lax.rem(d + k, DP)}, device_id_type=MESH)

    q = qt_ref[...]
    high = q.astype(BF16).astype(F32)
    qcat[...] = jnp.concatenate([high, q - high], axis=0).T.astype(BF16)

    load_blk.wait()
    part = dot(wblk[...].reshape(TP * PIECE, COLS), qcat[...])
    wq_send[...] = split(fold(part)).reshape(TP, PIECE, 128)
    wq_recv[t] = wq_send[t]

    pl.semaphore_wait(barrier, TP - 1 + DP - 1)

    def send_tp(i, src, dst):
        @pl.loop(1, TP)
        def _(k):
            peer = lax.rem(t + k, TP)
            pltpu.make_async_remote_copy(
                src(peer), dst, x_send.at[i], x_recv.at[i], device_id={"tp": peer}, device_id_type=MESH
            ).start()

    def send_dp(i, src, dst):
        @pl.loop(1, DP)
        def _(k):
            peer = lax.rem(d + k, DP)
            pltpu.make_async_remote_copy(
                src(peer), dst, x_send.at[i], x_recv.at[i], device_id={"dp": peer}, device_id_type=MESH
            ).start()

    def wait_all(sems, i, like):
        pltpu.make_async_copy(like, like, sems.at[i]).wait()

    sends = []

    def rows(h, i):
        return pl.ds(h * HALF + i * CUT, CUT)

    def ag(owner, h, i, dest, src=None):
        r = rows(h, i)
        copy = pltpu.make_async_remote_copy(
            abuf.at[owner, r] if src is None else src.at[r], abuf.at[owner, r],
            ag_send.at[len(sends)], ag_recv.at[owner, h, i],
            device_id={"tp": dest}, device_id_type=MESH,
        )
        copy.start()
        sends.append(copy)

    def arrived(owner, h, i):
        r = rows(h, i)
        pltpu.make_async_copy(abuf.at[owner, r], abuf.at[owner, r], ag_recv.at[owner, h, i]).wait()

    send_tp(0, lambda peer: wq_send.at[peer], wq_recv.at[t])
    for hh in range(2):
        for i in range(CUTS):
            ag(t, hh, i, up, a_hbm)
            ag(t, 1 - hh, i, down, a_hbm)
    for h in range(2):
        for i in range(CUTS):
            ag(t, h, i, sib, a_hbm)

    load_e.wait()

    @pl.loop(0, TP)
    def _(k):
        block = ev[pl.ds(pl.multiple_of(k * FEAT, FEAT), FEAT), :]
        eq_send[k] = split(fold(dot(block, qcat[...])))

    mine = pl.ds(pl.multiple_of(d * PIECE, PIECE), PIECE)

    def piece(peer):
        return pl.ds(pl.multiple_of(peer * PIECE, PIECE), PIECE)

    e_recv[d] = eq_send[:, mine, :]
    send_dp(1, lambda peer: eq_send.at[:, piece(peer)], e_recv.at[d])

    wait_all(x_recv, 0, wq_recv.at[pl.ds(0, TP - 1)])
    total = wq_recv[0].astype(F32)
    for k in range(1, TP):
        total += wq_recv[k].astype(F32)
    wq_full[mine, :] = split(fold(total))
    send_dp(2, lambda peer: wq_full.at[mine], wq_full.at[mine])

    load_res.wait()
    load_tch.wait()
    STEP = 256

    @pl.loop(0, TOK // STEP)
    def _(k):
        r = pl.ds(pl.multiple_of(k * STEP, STEP), STEP)
        xq[r, :] = dot(res[r, :], qcat[...]) - dot(tch[r, :], qcat[...])

    load_a.wait()
    load_w.wait()

    def take(owner, lo, n, first=False):
        @pl.loop(0, n // STEP)
        def _(k):
            r = pl.ds(pl.multiple_of(lo + k * STEP, STEP), STEP)
            block = abuf[owner, r, :]
            at[owner, :, r] = block.T
            term = dot(block, wv[owner])
            if first:
                proj[r, :] = term
            else:
                proj[r, :] += term

    take(t, 0, TOK, first=True)

    wait_all(x_recv, 2, wq_full.at[pl.ds(0, FEAT - PIECE)])

    @pl.loop(0, TOK // STEP)
    def _(k):
        r = pl.ds(pl.multiple_of(k * STEP, STEP), STEP)
        part = xq[r, :] + dot(abuf[t, r, :], wq_full[...])
        dq_send[r, :] = split(fold(part))

    def tokens(peer):
        return pl.ds(pl.multiple_of(peer * TOKP, TOKP), TOKP)

    dq_recv[t] = dq_send[tokens(t), :]
    send_tp(3, lambda peer: dq_send.at[tokens(peer)], dq_recv.at[t])

    for h in range(2):
        for i in range(CUTS):
            arrived(sib, h, i)
    take(sib, 0, TOK)

    wait_all(x_recv, 3, dq_recv.at[pl.ds(0, TP - 1)])
    total = dq_recv[0].astype(F32)
    for k in range(1, TP):
        total += dq_recv[k].astype(F32)
    dq_full[tokens(t), :] = split(fold(total))
    send_tp(4, lambda peer: dq_full.at[tokens(t)], dq_full.at[tokens(t)])

    for i in range(CUTS):
        arrived(down, 0, i)
        ag(down, 0, i, up)
        ag(down, 0, i, sib)
        arrived(up, 1, i)
        ag(up, 1, i, down)
        ag(up, 1, i, sib)

    wait_all(x_recv, 1, e_recv.at[pl.ds(0, DP - 1)])

    @pl.loop(0, TP)
    def _(k):
        total = e_recv[0, k].astype(F32)
        for j in range(1, DP):
            total += e_recv[j, k].astype(F32)
        e2_send[k] = split(fold(total))

    e2_recv[t] = e2_send[t]
    send_tp(5, lambda peer: e2_send.at[peer], e2_recv.at[t])

    wait_all(x_recv, 4, dq_full.at[pl.ds(0, TOK - TOKP)])
    part = dot(at[t], dq_full[...]) * (1.0 / 32.0)
    pa_send[...] = split(fold(part))
    pa_recv[d] = pa_send[mine, :]
    send_dp(6, lambda peer: pa_send.at[piece(peer)], pa_recv.at[d])

    take(down, 0, HALF)
    take(up, HALF, HALF)

    wait_all(x_recv, 5, e2_recv.at[pl.ds(0, TP - 1)])
    wait_all(x_recv, 6, pa_recv.at[pl.ds(0, DP - 1)])
    total = e2_recv[0].astype(F32)
    for k in range(1, TP):
        total += e2_recv[k].astype(F32)
    for k in range(DP):
        total += pa_recv[k].astype(F32)
    pfull[t, mine, :] = split(fold(total) * (1.0 / DP))
    send_tp(7, lambda peer: pfull.at[t, mine], pfull.at[t, mine])

    for i in range(CUTS):
        arrived(down, 1, i)
        ag(down, 1, i, sib)
        arrived(up, 0, i)
        ag(up, 0, i, sib)

    wait_all(x_recv, 7, pfull.at[0, pl.ds(0, (TP - 1) * PIECE)])
    send_dp(8, lambda peer: pfull.at[:, mine], pfull.at[:, mine])

    take(down, HALF, HALF)
    take(up, 0, HALF)
    for owner, h in ((other(down), 0), (other(up), 1), (other(down), 1), (other(up), 0)):
        for i in range(CUTS):
            arrived(owner, h, i)
        take(owner, h * HALF, HALF)

    for i in range(CUTS):
        arrived(far, 0, i)
        ag(far, 0, i, sib)
        arrived(far, 1, i)
        ag(far, 1, i, sib)
    take(far, 0, TOK)
    for h in range(2):
        for i in range(CUTS):
            arrived(other(far), h, i)
    take(other(far), 0, TOK)

    @pl.loop(0, TOK // STEP)
    def _(k):
        r = pl.ds(pl.multiple_of(k * STEP, STEP), STEP)
        res[r, :] = (res[r, :].astype(F32) + proj[r, :] - tch[r, :].astype(F32)).astype(BF16)

    wait_all(x_recv, 8, pfull.at[:, pl.ds(0, FEAT - PIECE)])

    proj[:, 0:128] = dot(abuf[0], pfull[0])

    @pl.loop(1, TP)
    def _(k):
        proj[:, 0:128] += dot(abuf[k], pfull[k])

    @pl.loop(0, TP)
    def _(k):
        pt[k] = pfull[k].T

    ap = fold(proj[:, 0:128]).T
    ap_high = ap.astype(BF16).astype(F32)
    sub = lax.broadcasted_iota(jnp.int32, ap.shape, 0)
    ap_cat = jnp.where(sub < RANK, ap_high, ap - ap_high).astype(BF16)
    right = dot(ap_cat, res[...]) * (1.0 / 32.0)
    gram = jnp.zeros((128, 128), F32)
    for k in range(TP):
        right += dot(pt[k], ev[k * FEAT : (k + 1) * FEAT, :])
        gram += dot(pt[k], pfull[k])
    right = right[0:RANK] + right[RANK:]
    for i in range(8):
        for j in range(5):
            r_send[i * 5 + j] = right[8 * i : 8 * i + 8, 128 * j : 128 * j + 128]
    for j in range(40, TILES):
        r_send[j] = jnp.zeros((8, 128), F32)
    PER = TILES // DP
    r_recv[d] = r_send[pl.ds(d * PER, PER)]
    send_dp(9, lambda peer: r_send.at[pl.ds(peer * PER, PER)], r_recv.at[d])

    def stored(k):
        r = pl.ds(pl.multiple_of(k * FEAT, FEAT), FEAT)
        return pltpu.make_async_copy(ev.at[r], m_hbm.at[r], out_sem.at[k])

    def matrix(k):
        for half in range(2):
            r = pl.ds(pl.multiple_of(k * FEAT + half * 256, 256), 256)
            grad = dot(at[k, half * 256 : half * 256 + 256, :], res[...]) * (1.0 / 32.0)
            ev[r, :] = (grad + ev[r, :].astype(F32)).astype(BF16)
        stored(k).start()

    pl.loop(0, TP // 2)(matrix)

    wait_all(x_recv, 9, r_recv.at[pl.ds(0, DP - 1)])
    total = r_recv[0]
    for k in range(1, DP):
        total += r_recv[k]
    r_full[pl.ds(d * PER, PER)] = total
    send_dp(10, lambda peer: r_full.at[pl.ds(d * PER, PER)], r_full.at[pl.ds(d * PER, PER)])

    linv = inverse_factor(fold(gram[0:RANK] + gram[RANK:]))
    lsplit = split(linv)
    lhigh = linv.astype(BF16).astype(F32)
    back = jnp.concatenate([lhigh, linv - lhigh], axis=0).T.astype(BF16)

    @pl.loop(0, TP)
    def _(k):
        r = pl.ds(pl.multiple_of(k * FEAT, FEAT), FEAT)
        phat_ref[r, :] = split(fold(dot(pfull[k], back)))

    pl.loop(TP // 2, TP)(matrix)

    wait_all(x_recv, 10, r_full.at[pl.ds(0, TILES - PER)])
    summed = jnp.concatenate(
        [jnp.concatenate([r_full[i * 5 + j] for j in range(5)], axis=1) for i in range(8)], axis=0
    )
    rhigh, rlow = split_rows(summed)
    qnext_ref[...] = (dot(lsplit, rhigh) + dot(lsplit, rlow)) * (1.0 / DP)

    for i, like in (
        (0, wq_recv.at[pl.ds(0, TP - 1)]),
        (1, e_recv.at[pl.ds(0, DP - 1)]),
        (2, wq_full.at[pl.ds(0, FEAT - PIECE)]),
        (3, dq_recv.at[pl.ds(0, TP - 1)]),
        (4, dq_full.at[pl.ds(0, TOK - TOKP)]),
        (5, e2_recv.at[pl.ds(0, TP - 1)]),
        (6, pa_recv.at[pl.ds(0, DP - 1)]),
        (7, pfull.at[0, pl.ds(0, (TP - 1) * PIECE)]),
        (8, pfull.at[:, pl.ds(0, FEAT - PIECE)]),
        (9, r_recv.at[pl.ds(0, DP - 1)]),
        (10, r_full.at[pl.ds(0, TILES - PER)]),
    ):
        wait_all(x_send, i, like)
    for copy in sends:
        copy.wait_send()

    @pl.loop(0, TP)
    def _(k):
        stored(k).wait()


def write_kernel(m_ref, phat_ref, qt_ref, out_ref, qout_ref):
    q = qt_ref[...]
    qhigh, qlow = split_rows(q)
    cat = phat_ref[...]
    approx = dot(jnp.concatenate([cat, cat], axis=1), jnp.concatenate([qhigh, qlow], axis=0))
    out_ref[...] = (m_ref[...].astype(F32) - approx).astype(BF16)
    qout_ref[...] = q


def per_device(attn_out, residual_in, teacher, out_weight, error_buf, q_start):
    any_space = pl.BlockSpec(memory_space=pl.ANY)
    vmem = pl.BlockSpec(memory_space=pltpu.VMEM)
    V, S = pltpu.VMEM, pltpu.SemaphoreType.DMA
    n_ag = CUTS * 2 * 7
    m, phat, qt = pl.pallas_call(
        main_kernel,
        name="gather_and_factors",
        out_shape=(
            jax.ShapeDtypeStruct((ROWS, COLS), BF16),
            jax.ShapeDtypeStruct((ROWS, 128), BF16),
            jax.ShapeDtypeStruct((RANK, COLS), F32),
        ),
        in_specs=[any_space] * 5 + [vmem],
        out_specs=(any_space, vmem, vmem),
        scratch_shapes=[
            V((TP, TOK, FEAT), BF16),
            V((TP, FEAT, TOK), BF16),
            V((TP, FEAT, COLS), BF16),
            V((ROWS, COLS), BF16),
            V((TOK, COLS), BF16),
            V((TOK, COLS), BF16),
            V((TOK, COLS), F32),
            V((TP, PIECE, COLS), BF16),
            V((COLS, 128), BF16),
            V((TOK, 128), F32),
            V((TP, PIECE, 128), BF16),
            V((TP, PIECE, 128), BF16),
            V((FEAT, 128), BF16),
            V((TOK, 128), BF16),
            V((TP, TOKP, 128), BF16),
            V((TOK, 128), BF16),
            V((FEAT, 128), BF16),
            V((DP, PIECE, 128), BF16),
            V((TP, FEAT, 128), BF16),
            V((DP, TP, PIECE, 128), BF16),
            V((TP, PIECE, 128), BF16),
            V((TP, PIECE, 128), BF16),
            V((TP, FEAT, 128), BF16),
            V((TP, 128, FEAT), BF16),
            V((TILES, 8, 128), F32),
            V((DP, TILES // DP, 8, 128), F32),
            V((TILES, 8, 128), F32),
            S((6,)),
            S((n_ag,)),
            S((TP, 2, CUTS)),
            S((11,)),
            S((11,)),
            S((TP,)),
        ],
        compiler_params=pltpu.CompilerParams(
            collective_id=0, has_side_effects=True, vmem_limit_bytes=60 * 2**20
        ),
    )(
        attn_out, residual_in, teacher,
        out_weight.reshape(TP, FEAT, COLS),
        error_buf[0], q_start.T,
    )
    block = 512
    error_next, q_next = pl.pallas_call(
        write_kernel,
        name="write_error",
        grid=(ROWS // block,),
        out_shape=(
            jax.ShapeDtypeStruct((ROWS, COLS), BF16),
            jax.ShapeDtypeStruct((RANK, COLS), F32),
        ),
        in_specs=[
            pl.BlockSpec((block, COLS), lambda i: (i, 0)),
            pl.BlockSpec((block, 128), lambda i: (i, 0)),
            pl.BlockSpec((RANK, COLS), lambda i: (0, 0)),
        ],
        out_specs=(
            pl.BlockSpec((block, COLS), lambda i: (i, 0)),
            pl.BlockSpec((RANK, COLS), lambda i: (0, 0)),
        ),
        compiler_params=pltpu.CompilerParams(vmem_limit_bytes=60 * 2**20),
    )(m, phat, qt)
    return error_next[None], q_next.T


def solution(mesh):
    return jax.shard_map(
        per_device,
        mesh=mesh,
        in_specs=(
            P("dp", "tp"),
            P("dp", "tp"),
            P("dp", "tp"),
            P(None, "tp"),
            P("dp", None, "tp"),
            P("tp", None),
        ),
        out_specs=(P("dp", None, "tp"), P("tp", None)),
        check_vma=False,
    )
```

```python
import jax
import jax.numpy as jnp
from jax import lax
from jax.experimental import pallas as pl
from jax.experimental.pallas import tpu as pltpu
from jax.sharding import PartitionSpec as P

MESH = pl.DeviceIdType.MESH
F32, BF16 = jnp.float32, jnp.bfloat16
DP, TP = 16, 8
TOK, FEAT, COLS, RANK = 1024, 512, 640, 64
ROWS = FEAT * TP
PIECE = FEAT // DP
TOKP = TOK // TP
HALF = TOK // 2
CUTS = 2
CUT = HALF // CUTS
TILES = 48


def dot(a, b):
    return jnp.dot(a, b, preferred_element_type=F32)


def fold(x):
    return x + pltpu.roll(x, RANK, 1)


def split(x):
    lane = lax.broadcasted_iota(jnp.int32, x.shape, 1)
    high = x.astype(BF16).astype(F32)
    return jnp.where(lane < RANK, high, x - high).astype(BF16)


def split_rows(x):
    high = x.astype(BF16).astype(F32)
    low = x - high
    return (
        jnp.concatenate([high, high], axis=0).astype(BF16),
        jnp.concatenate([low, low], axis=0).astype(BF16),
    )


def inverse_factor(gram):
    lane = lax.broadcasted_iota(jnp.int32, (8, 128), 1)
    sub = lax.broadcasted_iota(jnp.int32, (8, 128), 0)
    blocks = []
    for b in range(8):
        eye = jnp.where(lane == sub + (RANK + 8 * b), 1.0, 0.0)
        blocks.append(jnp.where(lane < RANK, gram[8 * b : 8 * b + 8, :], eye))
    for k in range(RANK):
        home, at = k // 8, k % 8
        pivot = jnp.broadcast_to(blocks[home][at : at + 1, :], (8, 128))
        scaled = pivot / jnp.broadcast_to(pivot[:, k : k + 1], (8, 128))
        for b in range(home, 8):
            column = jnp.broadcast_to(blocks[b][:, k : k + 1], (8, 128))
            if b == home:
                column = jnp.where(sub > at, column, 0.0)
            blocks[b] = blocks[b] - column * scaled
    out = []
    for b in range(8):
        diagonal = jnp.sum(jnp.where(lane == sub + 8 * b, blocks[b], 0.0), axis=1, keepdims=True)
        rows = jnp.where(lane < RANK, 0.0, blocks[b] * lax.rsqrt(diagonal))
        out.append(fold(rows))
    return jnp.concatenate(out, axis=0)


def main_kernel(
    a_hbm, res_hbm, tch_hbm, w_hbm, e_hbm, qt_ref,
    m_hbm, p_hbm, coef_ref, qnext_ref,
    abuf, at, wv, ev, res, tch, proj, wblk, qcat, xq,
    wq_send, wq_recv, wq_full, dq_send, dq_recv, dq_full,
    pa_send, pa_recv, eq_send, e0_recv, e1_send, e_recv, e2_send, e2_recv, pfull, pt,
    r_send, r_recv, r_full,
    load_sem, ag_send, ag_recv, x_send, x_recv, p_recv, out_sem,
):
    d, t = lax.axis_index("dp"), lax.axis_index("tp")
    y, c = t // 2, lax.rem(t, 2)
    sib = y * 2 + 1 - c
    up = lax.rem(y + 1, 4) * 2 + c
    down = lax.rem(y + 3, 4) * 2 + c
    far = lax.rem(y + 2, 4) * 2 + c
    odown, oup, ofar = (lax.rem(y + k, 4) * 2 + 1 - c for k in (3, 1, 2))

    mine = pl.ds(pl.multiple_of(d * PIECE, PIECE), PIECE)
    load_blk = pltpu.make_async_copy(w_hbm.at[:, mine], wblk, load_sem.at[0])
    load_a = pltpu.make_async_copy(a_hbm, abuf.at[t], load_sem.at[1])
    load_e = pltpu.make_async_copy(e_hbm, ev, load_sem.at[2])
    load_res = pltpu.make_async_copy(res_hbm, res, load_sem.at[3])
    load_tch = pltpu.make_async_copy(tch_hbm, tch, load_sem.at[4])
    load_w = pltpu.make_async_copy(w_hbm, wv, load_sem.at[5])
    for load in (load_blk, load_e, load_a, load_res, load_tch, load_w):
        load.start()

    barrier = pltpu.get_barrier_semaphore()

    @pl.loop(1, TP)
    def _(k):
        pl.semaphore_signal(barrier, inc=1, device_id={"tp": lax.rem(t + k, TP)}, device_id_type=MESH)

    @pl.loop(1, DP)
    def _(k):
        pl.semaphore_signal(barrier, inc=1, device_id={"dp": lax.rem(d + k, DP)}, device_id_type=MESH)

    q = qt_ref[...]
    high = q.astype(BF16).astype(F32)
    qcat[...] = jnp.concatenate([high, q - high], axis=0).T.astype(BF16)

    load_blk.wait()
    part = dot(wblk[...].reshape(TP * PIECE, COLS), qcat[...])
    wq_send[...] = split(fold(part)).reshape(TP, PIECE, 128)
    wq_recv[t] = wq_send[t]

    pl.semaphore_wait(barrier, TP - 1 + DP - 1)

    started = {}

    def remote(i, src, dst, peer, recv=None):
        pltpu.make_async_remote_copy(
            src, dst, x_send.at[i], x_recv.at[i] if recv is None else recv,
            device_id=peer, device_id_type=MESH,
        ).start()

    def send_tp(i, src, dst, like):
        started[i] = like

        @pl.loop(1, TP)
        def _(k):
            peer = lax.rem(t + k, TP)
            remote(i, src(peer), dst, {"tp": peer})

    def send_y(i, src, dst, like):
        started[i] = like

        @pl.loop(1, 4)
        def _(k):
            peer = lax.rem(y + k, 4)
            remote(i, src(peer), dst, {"tp": peer * 2 + c})

    def send_dp(i, src, dst, like, recv=None):
        started[i] = like

        @pl.loop(1, DP)
        def _(k):
            peer = lax.rem(d + k, DP)
            remote(i, src(peer), dst, {"dp": peer}, recv)

    def wait_all(i):
        pltpu.make_async_copy(started[i], started[i], x_recv.at[i]).wait()

    sends = []

    def rows(h, i):
        return pl.ds(h * HALF + i * CUT, CUT)

    def ag(owner, h, i, dest, src=None):
        r = rows(h, i)
        copy = pltpu.make_async_remote_copy(
            abuf.at[owner, r] if src is None else src.at[r], abuf.at[owner, r],
            ag_send.at[len(sends)], ag_recv.at[owner, h, i],
            device_id={"tp": dest}, device_id_type=MESH,
        )
        copy.start()
        sends.append(copy)

    def arrived(owner, h, i):
        r = rows(h, i)
        pltpu.make_async_copy(abuf.at[owner, r], abuf.at[owner, r], ag_recv.at[owner, h, i]).wait()

    send_tp(0, lambda peer: wq_send.at[peer], wq_recv.at[t], wq_recv.at[pl.ds(0, TP - 1)])
    for hh in range(2):
        for i in range(CUTS):
            ag(t, hh, i, up, a_hbm)
            ag(t, 1 - hh, i, down, a_hbm)

    load_e.wait()

    @pl.loop(0, TP)
    def _(k):
        block = ev[pl.ds(pl.multiple_of(k * FEAT, FEAT), FEAT), :]
        eq_send[k // 2, lax.rem(k, 2)] = split(fold(dot(block, qcat[...])))

    started[1] = e0_recv
    remote(1, eq_send.at[:, 1 - c], e0_recv, {"tp": sib})
    for h in range(2):
        for i in range(CUTS):
            ag(t, h, i, sib, a_hbm)

    def piece(peer):
        return pl.ds(pl.multiple_of(peer * PIECE, PIECE), PIECE)

    wait_all(0)
    total = wq_recv[0].astype(F32)
    for k in range(1, TP):
        total += wq_recv[k].astype(F32)
    wq_full[mine, :] = split(fold(total))
    send_dp(2, lambda peer: wq_full.at[mine], wq_full.at[mine], wq_full.at[pl.ds(0, FEAT - PIECE)])

    wait_all(1)

    @pl.loop(0, 4)
    def _(k):
        e1_send[k] = split(fold(eq_send[k, c].astype(F32) + e0_recv[k].astype(F32)))

    e_recv[d] = e1_send[:, mine, :]
    send_dp(5, lambda peer: e1_send.at[:, piece(peer)], e_recv.at[d], e_recv.at[pl.ds(0, DP - 1)])

    load_res.wait()
    load_tch.wait()
    STEP = 512

    @pl.loop(0, TOK // STEP)
    def _(k):
        r = pl.ds(pl.multiple_of(k * STEP, STEP), STEP)
        xq[r, :] = dot(res[r, :], qcat[...]) - dot(tch[r, :], qcat[...])

    load_a.wait()
    load_w.wait()

    def take(owner, lo, n, first=False):
        @pl.loop(0, n // STEP)
        def _(k):
            r = pl.ds(pl.multiple_of(lo + k * STEP, STEP), STEP)
            block = abuf[owner, r, :]
            at[owner, :, r] = block.T
            term = dot(block, wv[owner])
            if first:
                proj[r, :] = term
            else:
                proj[r, :] += term

    take(t, 0, TOK, first=True)

    wait_all(2)

    @pl.loop(0, TOK // STEP)
    def _(k):
        r = pl.ds(pl.multiple_of(k * STEP, STEP), STEP)
        part = xq[r, :] + dot(abuf[t, r, :], wq_full[...])
        dq_send[r, :] = split(fold(part))

    def tokens(peer):
        return pl.ds(pl.multiple_of(peer * TOKP, TOKP), TOKP)

    dq_recv[t] = dq_send[tokens(t), :]
    send_tp(3, lambda peer: dq_send.at[tokens(peer)], dq_recv.at[t], dq_recv.at[pl.ds(0, TP - 1)])

    for h in range(2):
        for i in range(CUTS):
            arrived(sib, h, i)
    take(sib, 0, TOK)

    wait_all(3)
    total = dq_recv[0].astype(F32)
    for k in range(1, TP):
        total += dq_recv[k].astype(F32)
    dq_full[tokens(t), :] = split(fold(total))
    send_tp(4, lambda peer: dq_full.at[tokens(t)], dq_full.at[tokens(t)], dq_full.at[pl.ds(0, TOK - TOKP)])

    for i in range(CUTS):
        arrived(down, 0, i)
        ag(down, 0, i, up)
        ag(down, 0, i, sib)
        arrived(up, 1, i)
        ag(up, 1, i, down)
        ag(up, 1, i, sib)

    wait_all(4)
    part = dot(at[t], dq_full[...]) * (1.0 / 32.0)
    pa_send[...] = split(fold(part))
    pa_recv[d] = pa_send[mine, :]
    send_dp(7, lambda peer: pa_send.at[piece(peer)], pa_recv.at[d], pa_recv.at[pl.ds(0, DP - 1)])

    wait_all(5)

    @pl.loop(0, 4)
    def _(k):
        total = e_recv[0, k].astype(F32)
        for j in range(1, DP):
            total += e_recv[j, k].astype(F32)
        e2_send[k] = split(fold(total))

    e2_recv[y] = e2_send[y]
    send_y(6, lambda peer: e2_send.at[peer], e2_recv.at[y], e2_recv.at[pl.ds(0, 3)])

    take(down, 0, HALF)
    take(up, HALF, HALF)

    wait_all(6)
    wait_all(7)
    total = e2_recv[0].astype(F32)
    for k in range(1, 4):
        total += e2_recv[k].astype(F32)
    for k in range(DP):
        total += pa_recv[k].astype(F32)
    pfull[y, c, mine, :] = split(fold(total) * (1.0 / DP))
    send_y(8, lambda peer: pfull.at[y, c, mine], pfull.at[y, c, mine], pfull.at[0, 0, pl.ds(0, 3 * PIECE)])

    for i in range(CUTS):
        arrived(down, 1, i)
        ag(down, 1, i, sib)
        arrived(up, 0, i)
        ag(up, 0, i, sib)

    wait_all(8)
    send_dp(9, lambda peer: pfull.at[:, c, mine], pfull.at[:, c, mine],
            pfull.at[:, 0, pl.ds(0, FEAT - PIECE)], p_recv.at[d])
    started[10] = pfull.at[:, 1 - c]
    remote(10, pfull.at[:, c, mine], pfull.at[:, c, mine], {"tp": sib})

    take(down, HALF, HALF)
    take(up, 0, HALF)
    for owner, h in ((odown, 0), (oup, 1), (odown, 1), (oup, 0)):
        for i in range(CUTS):
            arrived(owner, h, i)
        take(owner, h * HALF, HALF)

    @pl.loop(1, DP)
    def _(k):
        source = lax.rem(d + DP - k, DP)
        block = pfull.at[:, c, piece(source)]
        pltpu.make_async_copy(block, block, p_recv.at[source]).wait()
        remote(10, block, block, {"tp": sib})

    for i in range(CUTS):
        arrived(far, 0, i)
        ag(far, 0, i, sib)
        arrived(far, 1, i)
        ag(far, 1, i, sib)
    take(far, 0, TOK)

    wait_all(10)
    copy_p = pltpu.make_async_copy(pfull, p_hbm, out_sem.at[TP])
    copy_p.start()
    right = jnp.zeros((128, COLS), F32)
    gram = jnp.zeros((128, 128), F32)
    for k in range(TP):
        pt[k] = pfull[k // 2, k % 2].T
        right += dot(pt[k], ev[k * FEAT : (k + 1) * FEAT, :])
        gram += dot(pt[k], pfull[k // 2, k % 2])
    linv = inverse_factor(fold(gram[0:RANK] + gram[RANK:]))

    for h in range(2):
        for i in range(CUTS):
            arrived(ofar, h, i)
    take(ofar, 0, TOK)

    @pl.loop(0, TOK // STEP)
    def _(k):
        r = pl.ds(pl.multiple_of(k * STEP, STEP), STEP)
        res[r, :] = (res[r, :].astype(F32) + proj[r, :] - tch[r, :].astype(F32)).astype(BF16)

    ap = dot(pt[0], at[0])
    for k in range(1, TP):
        ap += dot(pt[k], at[k])
    ap = ap[0:RANK] + ap[RANK:]
    ap_high = ap.astype(BF16).astype(F32)
    ap_cat = jnp.concatenate([ap_high, ap - ap_high], axis=0).astype(BF16)
    right += dot(ap_cat, res[...]) * (1.0 / 32.0)
    right = right[0:RANK] + right[RANK:]
    for i in range(8):
        for j in range(5):
            r_send[i * 5 + j] = right[8 * i : 8 * i + 8, 128 * j : 128 * j + 128]
    for j in range(40, TILES):
        r_send[j] = jnp.zeros((8, 128), F32)
    PER = TILES // DP
    r_recv[d] = r_send[pl.ds(d * PER, PER)]
    send_dp(11, lambda peer: r_send.at[pl.ds(peer * PER, PER)], r_recv.at[d], r_recv.at[pl.ds(0, DP - 1)])

    def stored(k):
        r = pl.ds(pl.multiple_of(k * 2 * FEAT, 2 * FEAT), 2 * FEAT)
        return pltpu.make_async_copy(ev.at[r], m_hbm.at[r], out_sem.at[k])

    def matrix(k):
        r = pl.ds(pl.multiple_of(k * 2 * FEAT, 2 * FEAT), 2 * FEAT)
        grad = dot(at[pl.ds(2 * k, 2)].reshape(2 * FEAT, TOK), res[...]) * (1.0 / 32.0)
        ev[r, :] = (grad + ev[r, :].astype(F32)).astype(BF16)
        stored(k).start()

    pl.loop(0, 2)(matrix)

    wait_all(11)
    total = r_recv[0]
    for k in range(1, DP):
        total += r_recv[k]
    r_full[pl.ds(d * PER, PER)] = total
    send_dp(12, lambda peer: r_full.at[pl.ds(d * PER, PER)], r_full.at[pl.ds(d * PER, PER)],
            r_full.at[pl.ds(0, TILES - PER)])

    pl.loop(2, 4)(matrix)
    lhigh = linv.astype(BF16).astype(F32)
    lcat = split(linv)
    lhigh2 = lhigh.T
    ltcat = jnp.concatenate([lhigh2[0:RANK], (linv - lhigh).T[0:RANK]], axis=1).astype(BF16)

    wait_all(12)
    summed = jnp.concatenate(
        [jnp.concatenate([r_full[i * 5 + j] for j in range(5)], axis=1) for i in range(8)], axis=0
    )
    rhigh, rlow = split_rows(summed)
    qt = (dot(lcat, rhigh) + dot(lcat, rlow)) * (1.0 / DP)
    qnext_ref[...] = qt
    rhigh, rlow = split_rows(qt)
    coef = dot(ltcat, rhigh) + dot(ltcat, rlow)
    chigh, clow = split_rows(coef)
    coef_ref[...] = jnp.concatenate([chigh, clow], axis=0)

    for i, like in started.items():
        pltpu.make_async_copy(like, like, x_send.at[i]).wait()
    for copy in sends:
        copy.wait_send()
    copy_p.wait()

    @pl.loop(0, 4)
    def _(k):
        stored(k).wait()


CHUNKS = 8
CHUNK = ROWS // CHUNKS


def write_kernel(m_hbm, p_hbm, coef_ref, qt_ref, out_hbm, qout_ref, m, p, out, m_sem, p_sem, out_sem):
    def load(k):
        r = pl.ds(pl.multiple_of(k * CHUNK, CHUNK), CHUNK)
        return (
            pltpu.make_async_copy(m_hbm.at[r], m.at[r], m_sem.at[k]),
            pltpu.make_async_copy(p_hbm.at[k // 2, lax.rem(k, 2)], p.at[r], p_sem.at[k]),
        )

    def store(k):
        r = pl.ds(pl.multiple_of(k * CHUNK, CHUNK), CHUNK)
        return pltpu.make_async_copy(out.at[r], out_hbm.at[r], out_sem.at[k])

    @pl.loop(0, CHUNKS)
    def _(k):
        for copy in load(k):
            copy.start()

    qout_ref[...] = qt_ref[...]

    @pl.loop(0, CHUNKS)
    def _(k):
        for copy in load(k):
            copy.wait()
        r = pl.ds(pl.multiple_of(k * CHUNK, CHUNK), CHUNK)
        cat = p[r, :]
        approx = dot(jnp.concatenate([cat, cat], axis=1), coef_ref[...])
        out[r, :] = (m[r, :].astype(F32) - approx).astype(BF16)
        store(k).start()

    @pl.loop(0, CHUNKS)
    def _(k):
        store(k).wait()


def per_device(attn_out, residual_in, teacher, out_weight, error_buf, q_start):
    any_space = pl.BlockSpec(memory_space=pl.ANY)
    vmem = pl.BlockSpec(memory_space=pltpu.VMEM)
    V, S = pltpu.VMEM, pltpu.SemaphoreType.DMA
    n_ag = CUTS * 2 * 7
    m, p, coef, qt = pl.pallas_call(
        main_kernel,
        name="gather_and_factors",
        out_shape=(
            jax.ShapeDtypeStruct((ROWS, COLS), BF16),
            jax.ShapeDtypeStruct((4, 2, FEAT, 128), BF16),
            jax.ShapeDtypeStruct((256, COLS), BF16),
            jax.ShapeDtypeStruct((RANK, COLS), F32),
        ),
        in_specs=[any_space] * 5 + [vmem],
        out_specs=(any_space, any_space, vmem, vmem),
        scratch_shapes=[
            V((TP, TOK, FEAT), BF16),
            V((TP, FEAT, TOK), BF16),
            V((TP, FEAT, COLS), BF16),
            V((ROWS, COLS), BF16),
            V((TOK, COLS), BF16),
            V((TOK, COLS), BF16),
            V((TOK, COLS), F32),
            V((TP, PIECE, COLS), BF16),
            V((COLS, 128), BF16),
            V((TOK, 128), F32),
            V((TP, PIECE, 128), BF16),
            V((TP, PIECE, 128), BF16),
            V((FEAT, 128), BF16),
            V((TOK, 128), BF16),
            V((TP, TOKP, 128), BF16),
            V((TOK, 128), BF16),
            V((FEAT, 128), BF16),
            V((DP, PIECE, 128), BF16),
            V((4, 2, FEAT, 128), BF16),
            V((4, FEAT, 128), BF16),
            V((4, FEAT, 128), BF16),
            V((DP, 4, PIECE, 128), BF16),
            V((4, PIECE, 128), BF16),
            V((4, PIECE, 128), BF16),
            V((4, 2, FEAT, 128), BF16),
            V((TP, 128, FEAT), BF16),
            V((TILES, 8, 128), F32),
            V((DP, TILES // DP, 8, 128), F32),
            V((TILES, 8, 128), F32),
            S((6,)),
            S((n_ag,)),
            S((TP, 2, CUTS)),
            S((13,)),
            S((13,)),
            S((DP,)),
            S((TP + 1,)),
        ],
        compiler_params=pltpu.CompilerParams(
            collective_id=0, has_side_effects=True, vmem_limit_bytes=60 * 2**20
        ),
    )(
        attn_out, residual_in, teacher,
        out_weight.reshape(TP, FEAT, COLS),
        error_buf[0], q_start.T,
    )
    error_next, q_next = pl.pallas_call(
        write_kernel,
        name="write_error",
        out_shape=(
            jax.ShapeDtypeStruct((ROWS, COLS), BF16),
            jax.ShapeDtypeStruct((RANK, COLS), F32),
        ),
        in_specs=[any_space, any_space, vmem, vmem],
        out_specs=(any_space, vmem),
        scratch_shapes=[
            V((ROWS, COLS), BF16),
            V((ROWS, 128), BF16),
            V((ROWS, COLS), BF16),
            S((CHUNKS,)),
            S((CHUNKS,)),
            S((CHUNKS,)),
        ],
        compiler_params=pltpu.CompilerParams(vmem_limit_bytes=60 * 2**20),
    )(m, p, coef, qt)
    return error_next[None], q_next.T


def solution(mesh):
    return jax.shard_map(
        per_device,
        mesh=mesh,
        in_specs=(
            P("dp", "tp"),
            P("dp", "tp"),
            P("dp", "tp"),
            P(None, "tp"),
            P("dp", None, "tp"),
            P("tp", None),
        ),
        out_specs=(P("dp", None, "tp"), P("tp", None)),
        check_vma=False,
    )
```

```python
import jax
import jax.numpy as jnp
from jax import lax
from jax.experimental import pallas as pl
from jax.experimental.pallas import tpu as pltpu
from jax.sharding import PartitionSpec as P

MESH = pl.DeviceIdType.MESH
F32, BF16 = jnp.float32, jnp.bfloat16
DP, TP = 16, 8
TOK, FEAT, COLS, RANK = 1024, 512, 640, 64
ROWS = FEAT * TP
PIECE = FEAT // DP
TOKP = TOK // TP
HALF = TOK // 2
CUTS = 4
CUT = HALF // CUTS
TILES = 48
W2, W3 = 1, 1


def dot(a, b):
    return jnp.dot(a, b, preferred_element_type=F32)


def fold(x):
    return x + pltpu.roll(x, RANK, 1)


def split(x):
    lane = lax.broadcasted_iota(jnp.int32, x.shape, 1)
    high = x.astype(BF16).astype(F32)
    return jnp.where(lane < RANK, high, x - high).astype(BF16)


def split_rows(x):
    high = x.astype(BF16).astype(F32)
    low = x - high
    return (
        jnp.concatenate([high, high], axis=0).astype(BF16),
        jnp.concatenate([low, low], axis=0).astype(BF16),
    )


def inverse_factor(gram):
    lane = lax.broadcasted_iota(jnp.int32, (8, 128), 1)
    sub = lax.broadcasted_iota(jnp.int32, (8, 128), 0)
    blocks = []
    for b in range(8):
        eye = jnp.where(lane == sub + (RANK + 8 * b), 1.0, 0.0)
        blocks.append(jnp.where(lane < RANK, gram[8 * b : 8 * b + 8, :], eye))
    for k in range(RANK):
        home, at = k // 8, k % 8
        pivot = jnp.broadcast_to(blocks[home][at : at + 1, :], (8, 128))
        scaled = pivot / jnp.broadcast_to(pivot[:, k : k + 1], (8, 128))
        for b in range(home, 8):
            column = jnp.broadcast_to(blocks[b][:, k : k + 1], (8, 128))
            if b == home:
                column = jnp.where(sub > at, column, 0.0)
            blocks[b] = blocks[b] - column * scaled
    out = []
    for b in range(8):
        diagonal = jnp.sum(jnp.where(lane == sub + 8 * b, blocks[b], 0.0), axis=1, keepdims=True)
        rows = jnp.where(lane < RANK, 0.0, blocks[b] * lax.rsqrt(diagonal))
        out.append(fold(rows))
    return jnp.concatenate(out, axis=0)


def main_kernel(
    a_hbm, res_hbm, tch_hbm, w_hbm, e_hbm, qt_ref,
    m_hbm, p_hbm, coef_ref, qnext_ref,
    abuf, at, wv, ev, res, tch, proj, wblk, qcat, xq,
    wq_send, wq_recv, wq_full, dq_send, dq_recv, dq_full,
    pa_send, pa_recv, eq_send, e0_recv, e1_send, e_recv, e2_send, e2_recv, pfull, pt,
    r_send, r_recv, r_full,
    load_sem, ag_send, ag_recv, x_send, x_recv, p_recv, out_sem,
):
    d, t = lax.axis_index("dp"), lax.axis_index("tp")
    y, c = t // 2, lax.rem(t, 2)
    sib = y * 2 + 1 - c
    up = lax.rem(y + 1, 4) * 2 + c
    down = lax.rem(y + 3, 4) * 2 + c
    far = lax.rem(y + 2, 4) * 2 + c
    odown, oup, ofar = (lax.rem(y + k, 4) * 2 + 1 - c for k in (3, 1, 2))

    mine = pl.ds(pl.multiple_of(d * PIECE, PIECE), PIECE)
    load_blk = pltpu.make_async_copy(w_hbm.at[:, mine], wblk, load_sem.at[0])
    load_a = pltpu.make_async_copy(a_hbm, abuf.at[t], load_sem.at[1])
    load_e = pltpu.make_async_copy(e_hbm, ev, load_sem.at[2])
    load_res = pltpu.make_async_copy(res_hbm, res, load_sem.at[3])
    load_tch = pltpu.make_async_copy(tch_hbm, tch, load_sem.at[4])
    load_w = pltpu.make_async_copy(w_hbm, wv, load_sem.at[5])
    for load in (load_blk, load_res, load_tch, load_e, load_a, load_w):
        load.start()

    barrier = pltpu.get_barrier_semaphore()

    @pl.loop(1, TP)
    def _(k):
        pl.semaphore_signal(barrier, inc=1, device_id={"tp": lax.rem(t + k, TP)}, device_id_type=MESH)

    @pl.loop(1, DP)
    def _(k):
        pl.semaphore_signal(barrier, inc=1, device_id={"dp": lax.rem(d + k, DP)}, device_id_type=MESH)

    q = qt_ref[...]
    high = q.astype(BF16).astype(F32)
    qcat[...] = jnp.concatenate([high, q - high], axis=0).T.astype(BF16)

    load_blk.wait()
    part = dot(wblk[...].reshape(TP * PIECE, COLS), qcat[...])
    wq_send[...] = split(fold(part)).reshape(TP, PIECE, 128)
    wq_recv[t] = wq_send[t]

    load_res.wait()
    load_tch.wait()
    STEP = 512

    @pl.loop(0, TOK // STEP)
    def _(k):
        r = pl.ds(pl.multiple_of(k * STEP, STEP), STEP)
        xq[r, :] = dot(res[r, :], qcat[...]) - dot(tch[r, :], qcat[...])

    pl.semaphore_wait(barrier, TP - 1 + DP - 1)

    started = {}

    def remote(i, src, dst, peer, recv=None):
        pltpu.make_async_remote_copy(
            src, dst, x_send.at[i], x_recv.at[i] if recv is None else recv,
            device_id=peer, device_id_type=MESH,
        ).start()

    def send_tp(i, src, dst, like):
        started[i] = like

        @pl.loop(1, TP)
        def _(k):
            peer = lax.rem(t + k, TP)
            remote(i, src(peer), dst, {"tp": peer})

    def send_y(i, src, dst, like):
        started[i] = like

        @pl.loop(1, 4)
        def _(k):
            peer = lax.rem(y + k, 4)
            remote(i, src(peer), dst, {"tp": peer * 2 + c})

    def send_dp(i, src, dst, like, recv=None):
        started[i] = like

        @pl.loop(1, DP)
        def _(k):
            peer = lax.rem(d + k, DP)
            remote(i, src(peer), dst, {"dp": peer}, recv)

    def wait_all(i):
        pltpu.make_async_copy(started[i], started[i], x_recv.at[i]).wait()

    sends = []

    def rows(h, i, n=1):
        return pl.ds(h * HALF + i * CUT, n * CUT)

    def ag(owner, h, i, dest, src=None, n=1):
        r = rows(h, i, n)
        copy = pltpu.make_async_remote_copy(
            abuf.at[owner, r] if src is None else src.at[r], abuf.at[owner, r],
            ag_send.at[len(sends)], ag_recv.at[owner, h, i],
            device_id={"tp": dest}, device_id_type=MESH,
        )
        copy.start()
        sends.append(copy)

    def arrived(owner, h, i, n=1):
        r = rows(h, i, n)
        pltpu.make_async_copy(abuf.at[owner, r], abuf.at[owner, r], ag_recv.at[owner, h, i]).wait()

    def own(hh, pieces):
        for i in pieces:
            ag(t, hh, i, up, a_hbm)
            ag(t, 1 - hh, i, down, a_hbm)

    def pass_on(pieces):
        for i in pieces:
            ag(down, 0, i, up)
            ag(up, 1, i, down)

    send_tp(0, lambda peer: wq_send.at[peer], wq_recv.at[t], wq_recv.at[pl.ds(0, TP - 1)])
    own(0, range(CUTS))

    load_e.wait()

    @pl.loop(0, TP)
    def _(k):
        block = ev[pl.ds(pl.multiple_of(k * FEAT, FEAT), FEAT), :]
        eq_send[k // 2, lax.rem(k, 2)] = split(fold(dot(block, qcat[...])))

    started[1] = e0_recv
    remote(1, eq_send.at[:, 1 - c], e0_recv, {"tp": sib})
    for h in range(2):
        ag(t, h, 0, sib, a_hbm, CUTS)

    def piece(peer):
        return pl.ds(pl.multiple_of(peer * PIECE, PIECE), PIECE)

    wait_all(0)
    total = wq_recv[0].astype(F32)
    for k in range(1, TP):
        total += wq_recv[k].astype(F32)
    wq_full[mine, :] = split(fold(total))
    send_dp(2, lambda peer: wq_full.at[mine], wq_full.at[mine], wq_full.at[pl.ds(0, FEAT - PIECE)])

    wait_all(1)

    @pl.loop(0, 4)
    def _(k):
        e1_send[k] = split(fold(eq_send[k, c].astype(F32) + e0_recv[k].astype(F32)))

    e_recv[d] = e1_send[:, mine, :]
    send_dp(5, lambda peer: e1_send.at[:, piece(peer)], e_recv.at[d], e_recv.at[pl.ds(0, DP - 1)])

    load_a.wait()
    load_w.wait()

    def take(owner, lo, n, first=False):
        @pl.loop(0, n // STEP)
        def _(k):
            r = pl.ds(pl.multiple_of(lo + k * STEP, STEP), STEP)
            block = abuf[owner, r, :]
            at[owner, :, r] = block.T
            term = dot(block, wv[owner])
            if first:
                proj[r, :] = term
            else:
                proj[r, :] += term

    take(t, 0, TOK, first=True)

    wait_all(2)

    @pl.loop(0, TOK // STEP)
    def _(k):
        r = pl.ds(pl.multiple_of(k * STEP, STEP), STEP)
        part = xq[r, :] + dot(abuf[t, r, :], wq_full[...])
        dq_send[r, :] = split(fold(part))

    def tokens(peer):
        return pl.ds(pl.multiple_of(peer * TOKP, TOKP), TOKP)

    dq_recv[t] = dq_send[tokens(t), :]
    send_tp(3, lambda peer: dq_send.at[tokens(peer)], dq_recv.at[t], dq_recv.at[pl.ds(0, TP - 1)])

    own(1, range(0, W2))
    for h in range(2):
        arrived(sib, h, 0, CUTS)
    take(sib, 0, TOK)
    for owner, h in ((down, 0), (up, 1)):
        for i in range(CUTS):
            arrived(owner, h, i)
        ag(owner, h, 0, sib, None, CUTS)
        take(owner, h * HALF, HALF)

    wait_all(5)

    @pl.loop(0, 4)
    def _(k):
        total = e_recv[0, k].astype(F32)
        for j in range(1, DP):
            total += e_recv[j, k].astype(F32)
        e2_send[k] = split(fold(total))

    e2_recv[y] = e2_send[y]

    wait_all(3)
    total = dq_recv[0].astype(F32)
    for k in range(1, TP):
        total += dq_recv[k].astype(F32)
    dq_full[tokens(t), :] = split(fold(total))
    send_tp(4, lambda peer: dq_full.at[tokens(t)], dq_full.at[tokens(t)], dq_full.at[pl.ds(0, TOK - TOKP)])

    send_y(6, lambda peer: e2_send.at[peer], e2_recv.at[y], e2_recv.at[pl.ds(0, 3)])
    own(1, range(W2, CUTS))
    pass_on(range(0, W3))
    for owner, h in ((odown, 0), (oup, 1)):
        arrived(owner, h, 0, CUTS)
        take(owner, h * HALF, HALF)

    wait_all(4)
    part = dot(at[t], dq_full[...]) * (1.0 / 32.0)
    pa_send[...] = split(fold(part))
    pa_recv[d] = pa_send[mine, :]
    send_dp(7, lambda peer: pa_send.at[piece(peer)], pa_recv.at[d], pa_recv.at[pl.ds(0, DP - 1)])

    wait_all(6)
    wait_all(7)
    total = e2_recv[0].astype(F32)
    for k in range(1, 4):
        total += e2_recv[k].astype(F32)
    for k in range(DP):
        total += pa_recv[k].astype(F32)
    pfull[y, c, mine, :] = split(fold(total) * (1.0 / DP))
    send_y(8, lambda peer: pfull.at[y, c, mine], pfull.at[y, c, mine], pfull.at[0, 0, pl.ds(0, 3 * PIECE)])

    pass_on(range(W3, CUTS))
    for owner, h in ((down, 1), (up, 0)):
        for i in range(CUTS):
            arrived(owner, h, i)
        ag(owner, h, 0, sib, None, CUTS)
        take(owner, h * HALF, HALF)

    wait_all(8)
    send_dp(9, lambda peer: pfull.at[:, c, mine], pfull.at[:, c, mine],
            pfull.at[:, 0, pl.ds(0, FEAT - PIECE)], p_recv.at[d])
    started[10] = pfull.at[:, 1 - c]
    remote(10, pfull.at[:, c, mine], pfull.at[:, c, mine], {"tp": sib})

    for owner, h in ((odown, 1), (oup, 0)):
        arrived(owner, h, 0, CUTS)
        take(owner, h * HALF, HALF)

    @pl.loop(1, DP)
    def _(k):
        source = lax.rem(d + DP - k, DP)
        block = pfull.at[:, c, piece(source)]
        pltpu.make_async_copy(block, block, p_recv.at[source]).wait()
        remote(10, block, block, {"tp": sib})

    for i in range(0, CUTS, 2):
        for h in range(2):
            arrived(far, h, i)
            arrived(far, h, i + 1)
            ag(far, h, i, sib, None, 2)
    take(far, 0, TOK)

    wait_all(10)
    copy_p = pltpu.make_async_copy(pfull, p_hbm, out_sem.at[TP])
    copy_p.start()
    right = jnp.zeros((128, COLS), F32)
    gram = jnp.zeros((128, 128), F32)
    for k in range(TP):
        pt[k] = pfull[k // 2, k % 2].T
        right += dot(pt[k], ev[k * FEAT : (k + 1) * FEAT, :])
        gram += dot(pt[k], pfull[k // 2, k % 2])
    linv = inverse_factor(fold(gram[0:RANK] + gram[RANK:]))

    for i in range(0, CUTS, 2):
        for h in range(2):
            arrived(ofar, h, i, 2)
    take(ofar, 0, TOK)

    @pl.loop(0, TOK // STEP)
    def _(k):
        r = pl.ds(pl.multiple_of(k * STEP, STEP), STEP)
        res[r, :] = (res[r, :].astype(F32) + proj[r, :] - tch[r, :].astype(F32)).astype(BF16)

    ap = dot(pt[0], at[0])
    for k in range(1, TP):
        ap += dot(pt[k], at[k])
    ap = ap[0:RANK] + ap[RANK:]
    ap_high = ap.astype(BF16).astype(F32)
    ap_cat = jnp.concatenate([ap_high, ap - ap_high], axis=0).astype(BF16)
    right += dot(ap_cat, res[...]) * (1.0 / 32.0)
    right = right[0:RANK] + right[RANK:]
    for i in range(8):
        for j in range(5):
            r_send[i * 5 + j] = right[8 * i : 8 * i + 8, 128 * j : 128 * j + 128]
    for j in range(40, TILES):
        r_send[j] = jnp.zeros((8, 128), F32)
    PER = TILES // DP
    r_recv[d] = r_send[pl.ds(d * PER, PER)]
    send_dp(11, lambda peer: r_send.at[pl.ds(peer * PER, PER)], r_recv.at[d], r_recv.at[pl.ds(0, DP - 1)])

    def stored(k):
        r = pl.ds(pl.multiple_of(k * 2 * FEAT, 2 * FEAT), 2 * FEAT)
        return pltpu.make_async_copy(ev.at[r], m_hbm.at[r], out_sem.at[k])

    def matrix(k):
        r = pl.ds(pl.multiple_of(k * 2 * FEAT, 2 * FEAT), 2 * FEAT)
        grad = dot(at[pl.ds(2 * k, 2)].reshape(2 * FEAT, TOK), res[...]) * (1.0 / 32.0)
        ev[r, :] = (grad + ev[r, :].astype(F32)).astype(BF16)
        stored(k).start()

    pl.loop(0, 2)(matrix)

    wait_all(11)
    total = r_recv[0]
    for k in range(1, DP):
        total += r_recv[k]
    r_full[pl.ds(d * PER, PER)] = total
    send_dp(12, lambda peer: r_full.at[pl.ds(d * PER, PER)], r_full.at[pl.ds(d * PER, PER)],
            r_full.at[pl.ds(0, TILES - PER)])

    pl.loop(2, 4)(matrix)
    lhigh = linv.astype(BF16).astype(F32)
    lcat = split(linv)
    lhigh2 = lhigh.T
    ltcat = jnp.concatenate([lhigh2[0:RANK], (linv - lhigh).T[0:RANK]], axis=1).astype(BF16)

    wait_all(12)
    summed = jnp.concatenate(
        [jnp.concatenate([r_full[i * 5 + j] for j in range(5)], axis=1) for i in range(8)], axis=0
    )
    rhigh, rlow = split_rows(summed)
    qt = (dot(lcat, rhigh) + dot(lcat, rlow)) * (1.0 / DP)
    qnext_ref[...] = qt
    rhigh, rlow = split_rows(qt)
    coef = dot(ltcat, rhigh) + dot(ltcat, rlow)
    chigh, clow = split_rows(coef)
    coef_ref[...] = jnp.concatenate([chigh, clow], axis=0)

    for i, like in started.items():
        pltpu.make_async_copy(like, like, x_send.at[i]).wait()
    for copy in sends:
        copy.wait_send()
    copy_p.wait()

    @pl.loop(0, 4)
    def _(k):
        stored(k).wait()


CHUNKS = 8
CHUNK = ROWS // CHUNKS


def write_kernel(m_hbm, p_hbm, coef_ref, qt_ref, out_hbm, qout_ref, m, p, out, m_sem, p_sem, out_sem):
    def load(k):
        r = pl.ds(pl.multiple_of(k * CHUNK, CHUNK), CHUNK)
        return (
            pltpu.make_async_copy(m_hbm.at[r], m.at[r], m_sem.at[k]),
            pltpu.make_async_copy(p_hbm.at[k // 2, lax.rem(k, 2)], p.at[r], p_sem.at[k]),
        )

    def store(k):
        r = pl.ds(pl.multiple_of(k * CHUNK, CHUNK), CHUNK)
        return pltpu.make_async_copy(out.at[r], out_hbm.at[r], out_sem.at[k])

    @pl.loop(0, CHUNKS)
    def _(k):
        for copy in load(k):
            copy.start()

    qout_ref[...] = qt_ref[...]

    @pl.loop(0, CHUNKS)
    def _(k):
        for copy in load(k):
            copy.wait()
        r = pl.ds(pl.multiple_of(k * CHUNK, CHUNK), CHUNK)
        cat = p[r, :]
        approx = dot(jnp.concatenate([cat, cat], axis=1), coef_ref[...])
        out[r, :] = (m[r, :].astype(F32) - approx).astype(BF16)
        store(k).start()

    @pl.loop(0, CHUNKS)
    def _(k):
        store(k).wait()


def per_device(attn_out, residual_in, teacher, out_weight, error_buf, q_start):
    any_space = pl.BlockSpec(memory_space=pl.ANY)
    vmem = pl.BlockSpec(memory_space=pltpu.VMEM)
    V, S = pltpu.VMEM, pltpu.SemaphoreType.DMA
    n_ag = CUTS * 2 * 3 + 2 * 5 + 2
    m, p, coef, qt = pl.pallas_call(
        main_kernel,
        name="gather_and_factors",
        out_shape=(
            jax.ShapeDtypeStruct((ROWS, COLS), BF16),
            jax.ShapeDtypeStruct((4, 2, FEAT, 128), BF16),
            jax.ShapeDtypeStruct((256, COLS), BF16),
            jax.ShapeDtypeStruct((RANK, COLS), F32),
        ),
        in_specs=[any_space] * 5 + [vmem],
        out_specs=(any_space, any_space, vmem, vmem),
        scratch_shapes=[
            V((TP, TOK, FEAT), BF16),
            V((TP, FEAT, TOK), BF16),
            V((TP, FEAT, COLS), BF16),
            V((ROWS, COLS), BF16),
            V((TOK, COLS), BF16),
            V((TOK, COLS), BF16),
            V((TOK, COLS), F32),
            V((TP, PIECE, COLS), BF16),
            V((COLS, 128), BF16),
            V((TOK, 128), F32),
            V((TP, PIECE, 128), BF16),
            V((TP, PIECE, 128), BF16),
            V((FEAT, 128), BF16),
            V((TOK, 128), BF16),
            V((TP, TOKP, 128), BF16),
            V((TOK, 128), BF16),
            V((FEAT, 128), BF16),
            V((DP, PIECE, 128), BF16),
            V((4, 2, FEAT, 128), BF16),
            V((4, FEAT, 128), BF16),
            V((4, FEAT, 128), BF16),
            V((DP, 4, PIECE, 128), BF16),
            V((4, PIECE, 128), BF16),
            V((4, PIECE, 128), BF16),
            V((4, 2, FEAT, 128), BF16),
            V((TP, 128, FEAT), BF16),
            V((TILES, 8, 128), F32),
            V((DP, TILES // DP, 8, 128), F32),
            V((TILES, 8, 128), F32),
            S((6,)),
            S((n_ag,)),
            S((TP, 2, CUTS)),
            S((13,)),
            S((13,)),
            S((DP,)),
            S((TP + 1,)),
        ],
        compiler_params=pltpu.CompilerParams(
            collective_id=0, has_side_effects=True, vmem_limit_bytes=60 * 2**20
        ),
    )(
        attn_out, residual_in, teacher,
        out_weight.reshape(TP, FEAT, COLS),
        error_buf[0], q_start.T,
    )
    error_next, q_next = pl.pallas_call(
        write_kernel,
        name="write_error",
        out_shape=(
            jax.ShapeDtypeStruct((ROWS, COLS), BF16),
            jax.ShapeDtypeStruct((RANK, COLS), F32),
        ),
        in_specs=[any_space, any_space, vmem, vmem],
        out_specs=(any_space, vmem),
        scratch_shapes=[
            V((ROWS, COLS), BF16),
            V((ROWS, 128), BF16),
            V((ROWS, COLS), BF16),
            S((CHUNKS,)),
            S((CHUNKS,)),
            S((CHUNKS,)),
        ],
        compiler_params=pltpu.CompilerParams(vmem_limit_bytes=60 * 2**20),
    )(m, p, coef, qt)
    return error_next[None], q_next.T


def solution(mesh):
    return jax.shard_map(
        per_device,
        mesh=mesh,
        in_specs=(
            P("dp", "tp"),
            P("dp", "tp"),
            P("dp", "tp"),
            P(None, "tp"),
            P("dp", None, "tp"),
            P("tp", None),
        ),
        out_specs=(P("dp", None, "tp"), P("tp", None)),
        check_vma=False,
    )
```

```python
import jax
import jax.numpy as jnp
from jax import lax
from jax.experimental import pallas as pl
from jax.experimental.pallas import tpu as pltpu
from jax.sharding import PartitionSpec as P

MESH = pl.DeviceIdType.MESH
F32, BF16 = jnp.float32, jnp.bfloat16
DP, TP = 16, 8
TOK, FEAT, COLS, RANK = 1024, 512, 640, 64
ROWS = FEAT * TP
PIECE = FEAT // DP
TOKP = TOK // TP
HALF = TOK // 2
CUTS = 4
GROUP = 4
CUT = HALF // CUTS
TILES = 48
W2, W3 = 1, 1


def dot(a, b):
    return jnp.dot(a, b, preferred_element_type=F32)


def fold(x):
    return x + pltpu.roll(x, RANK, 1)


def split(x):
    lane = lax.broadcasted_iota(jnp.int32, x.shape, 1)
    high = x.astype(BF16).astype(F32)
    return jnp.where(lane < RANK, high, x - high).astype(BF16)


def split_rows(x):
    high = x.astype(BF16).astype(F32)
    low = x - high
    return (
        jnp.concatenate([high, high], axis=0).astype(BF16),
        jnp.concatenate([low, low], axis=0).astype(BF16),
    )


def inverse_factor(gram):
    lane = lax.broadcasted_iota(jnp.int32, (8, 128), 1)
    sub = lax.broadcasted_iota(jnp.int32, (8, 128), 0)
    blocks = []
    for b in range(8):
        eye = jnp.where(lane == sub + (RANK + 8 * b), 1.0, 0.0)
        blocks.append(jnp.where(lane < RANK, gram[8 * b : 8 * b + 8, :], eye))
    for k in range(0, RANK, GROUP):
        home, at = k // 8, k % 8
        span = range(GROUP)
        row = [jnp.broadcast_to(blocks[home][at + i : at + i + 1, :], (8, 128)) for i in span]
        small = [[jnp.broadcast_to(row[i][:, k + j : k + j + 1], (8, 128)) for j in span] for i in span]
        column = {
            b: [jnp.broadcast_to(blocks[b][:, k + j : k + j + 1], (8, 128)) for j in span] for b in range(home, 8)
        }
        for i in span:
            inverse = 1.0 / small[i][i]
            for j in range(i + 1, GROUP):
                factor = small[i][j] * inverse
                row[j] = row[j] - factor * row[i]
                for l in range(i + 1, GROUP):
                    small[j][l] = small[j][l] - factor * small[i][l]
                for b in column:
                    column[b][j] = column[b][j] - factor * column[b][i]
            row[i] = row[i] * inverse
        for b in column:
            for i in span:
                below = column[b][i]
                if b == home:
                    below = jnp.where(sub > at + i, below, 0.0)
                blocks[b] = blocks[b] - below * row[i]
    out = []
    for b in range(8):
        diagonal = jnp.sum(jnp.where(lane == sub + 8 * b, blocks[b], 0.0), axis=1, keepdims=True)
        rows = jnp.where(lane < RANK, 0.0, blocks[b] * lax.rsqrt(diagonal))
        out.append(fold(rows))
    return jnp.concatenate(out, axis=0)


def main_kernel(
    a_hbm, res_hbm, tch_hbm, w_hbm, e_hbm, qt_ref,
    m_hbm, p_hbm, coef_ref, qnext_ref,
    abuf, at, wv, ev, res, tch, proj, wblk, qcat, xq,
    wq_send, wq_recv, wq_full, dq_send, dq_recv, dq_full,
    pa_send, pa_recv, eq_send, e0_recv, e1_send, e_recv, e2_send, e2_recv, pfull, pt,
    r_send, r_recv, r_full,
    load_sem, ag_send, ag_recv, x_send, x_recv, p_recv, out_sem,
):
    d, t = lax.axis_index("dp"), lax.axis_index("tp")
    y, c = t // 2, lax.rem(t, 2)
    sib = y * 2 + 1 - c
    up = lax.rem(y + 1, 4) * 2 + c
    down = lax.rem(y + 3, 4) * 2 + c
    far = lax.rem(y + 2, 4) * 2 + c
    odown, oup, ofar = (lax.rem(y + k, 4) * 2 + 1 - c for k in (3, 1, 2))

    mine = pl.ds(pl.multiple_of(d * PIECE, PIECE), PIECE)
    load_blk = pltpu.make_async_copy(w_hbm.at[:, mine], wblk, load_sem.at[0])
    load_a = pltpu.make_async_copy(a_hbm, abuf.at[t], load_sem.at[1])
    load_e = pltpu.make_async_copy(e_hbm, ev, load_sem.at[2])
    load_res = pltpu.make_async_copy(res_hbm, res, load_sem.at[3])
    load_tch = pltpu.make_async_copy(tch_hbm, tch, load_sem.at[4])
    load_w = pltpu.make_async_copy(w_hbm, wv, load_sem.at[5])
    for load in (load_blk, load_res, load_tch, load_e, load_a, load_w):
        load.start()

    barrier = pltpu.get_barrier_semaphore()

    @pl.loop(1, TP)
    def _(k):
        pl.semaphore_signal(barrier, inc=1, device_id={"tp": lax.rem(t + k, TP)}, device_id_type=MESH)

    @pl.loop(1, DP)
    def _(k):
        pl.semaphore_signal(barrier, inc=1, device_id={"dp": lax.rem(d + k, DP)}, device_id_type=MESH)

    q = qt_ref[...]
    high = q.astype(BF16).astype(F32)
    qcat[...] = jnp.concatenate([high, q - high], axis=0).T.astype(BF16)

    load_blk.wait()
    part = dot(wblk[...].reshape(TP * PIECE, COLS), qcat[...])
    wq_send[...] = split(fold(part)).reshape(TP, PIECE, 128)
    wq_recv[t] = wq_send[t]

    load_res.wait()
    load_tch.wait()
    STEP = 512

    @pl.loop(0, TOK // STEP)
    def _(k):
        r = pl.ds(pl.multiple_of(k * STEP, STEP), STEP)
        xq[r, :] = dot(res[r, :], qcat[...]) - dot(tch[r, :], qcat[...])

    pl.semaphore_wait(barrier, TP - 1 + DP - 1)

    started = {}

    def remote(i, src, dst, peer, recv=None):
        pltpu.make_async_remote_copy(
            src, dst, x_send.at[i], x_recv.at[i] if recv is None else recv,
            device_id=peer, device_id_type=MESH,
        ).start()

    def send_tp(i, src, dst, like):
        started[i] = like

        @pl.loop(1, TP)
        def _(k):
            peer = lax.rem(t + k, TP)
            remote(i, src(peer), dst, {"tp": peer})

    def send_y(i, src, dst, like):
        started[i] = like

        @pl.loop(1, 4)
        def _(k):
            peer = lax.rem(y + k, 4)
            remote(i, src(peer), dst, {"tp": peer * 2 + c})

    def send_dp(i, src, dst, like, recv=None):
        started[i] = like

        @pl.loop(1, DP)
        def _(k):
            peer = lax.rem(d + k, DP)
            remote(i, src(peer), dst, {"dp": peer}, recv)

    def wait_all(i):
        pltpu.make_async_copy(started[i], started[i], x_recv.at[i]).wait()

    sends = []

    def rows(h, i, n=1):
        return pl.ds(h * HALF + i * CUT, n * CUT)

    def ag(owner, h, i, dest, src=None, n=1):
        r = rows(h, i, n)
        copy = pltpu.make_async_remote_copy(
            abuf.at[owner, r] if src is None else src.at[r], abuf.at[owner, r],
            ag_send.at[len(sends)], ag_recv.at[owner, h, i],
            device_id={"tp": dest}, device_id_type=MESH,
        )
        copy.start()
        sends.append(copy)

    def arrived(owner, h, i, n=1):
        r = rows(h, i, n)
        pltpu.make_async_copy(abuf.at[owner, r], abuf.at[owner, r], ag_recv.at[owner, h, i]).wait()

    def own(hh, pieces):
        for i in pieces:
            ag(t, hh, i, up, a_hbm)
            ag(t, 1 - hh, i, down, a_hbm)

    def pass_on(pieces):
        for i in pieces:
            ag(down, 0, i, up)
            ag(up, 1, i, down)

    send_tp(0, lambda peer: wq_send.at[peer], wq_recv.at[t], wq_recv.at[pl.ds(0, TP - 1)])
    own(0, range(CUTS))

    load_e.wait()

    @pl.loop(0, TP)
    def _(k):
        block = ev[pl.ds(pl.multiple_of(k * FEAT, FEAT), FEAT), :]
        eq_send[k // 2, lax.rem(k, 2)] = split(fold(dot(block, qcat[...])))

    started[1] = e0_recv
    remote(1, eq_send.at[:, 1 - c], e0_recv, {"tp": sib})
    for h in range(2):
        ag(t, h, 0, sib, a_hbm, CUTS)

    def piece(peer):
        return pl.ds(pl.multiple_of(peer * PIECE, PIECE), PIECE)

    wait_all(0)
    total = wq_recv[0].astype(F32)
    for k in range(1, TP):
        total += wq_recv[k].astype(F32)
    wq_full[mine, :] = split(fold(total))
    send_dp(2, lambda peer: wq_full.at[mine], wq_full.at[mine], wq_full.at[pl.ds(0, FEAT - PIECE)])

    wait_all(1)

    @pl.loop(0, 4)
    def _(k):
        e1_send[k] = split(fold(eq_send[k, c].astype(F32) + e0_recv[k].astype(F32)))

    e_recv[d] = e1_send[:, mine, :]
    send_dp(5, lambda peer: e1_send.at[:, piece(peer)], e_recv.at[d], e_recv.at[pl.ds(0, DP - 1)])

    load_a.wait()
    load_w.wait()

    def take(owner, lo, n, first=False):
        @pl.loop(0, n // STEP)
        def _(k):
            r = pl.ds(pl.multiple_of(lo + k * STEP, STEP), STEP)
            block = abuf[owner, r, :]
            at[owner, :, r] = block.T
            term = dot(block, wv[owner])
            if first:
                proj[r, :] = term
            else:
                proj[r, :] += term

    take(t, 0, TOK, first=True)

    wait_all(2)

    @pl.loop(0, TOK // STEP)
    def _(k):
        r = pl.ds(pl.multiple_of(k * STEP, STEP), STEP)
        part = xq[r, :] + dot(abuf[t, r, :], wq_full[...])
        dq_send[r, :] = split(fold(part))

    def tokens(peer):
        return pl.ds(pl.multiple_of(peer * TOKP, TOKP), TOKP)

    dq_recv[t] = dq_send[tokens(t), :]
    send_tp(3, lambda peer: dq_send.at[tokens(peer)], dq_recv.at[t], dq_recv.at[pl.ds(0, TP - 1)])

    own(1, range(0, W2))
    for h in range(2):
        arrived(sib, h, 0, CUTS)
    take(sib, 0, TOK)
    for owner, h in ((down, 0), (up, 1)):
        for i in range(CUTS):
            arrived(owner, h, i)
        ag(owner, h, 0, sib, None, CUTS)
        take(owner, h * HALF, HALF)

    wait_all(5)

    @pl.loop(0, 4)
    def _(k):
        total = e_recv[0, k].astype(F32)
        for j in range(1, DP):
            total += e_recv[j, k].astype(F32)
        e2_send[k] = split(fold(total))

    e2_recv[y] = e2_send[y]

    wait_all(3)
    total = dq_recv[0].astype(F32)
    for k in range(1, TP):
        total += dq_recv[k].astype(F32)
    dq_full[tokens(t), :] = split(fold(total))
    send_tp(4, lambda peer: dq_full.at[tokens(t)], dq_full.at[tokens(t)], dq_full.at[pl.ds(0, TOK - TOKP)])

    send_y(6, lambda peer: e2_send.at[peer], e2_recv.at[y], e2_recv.at[pl.ds(0, 3)])
    own(1, range(W2, CUTS))
    pass_on(range(0, W3))
    for owner, h in ((odown, 0), (oup, 1)):
        arrived(owner, h, 0, CUTS)
        take(owner, h * HALF, HALF)

    wait_all(4)
    part = dot(at[t], dq_full[...]) * (1.0 / 32.0)
    pa_send[...] = split(fold(part))
    pa_recv[d] = pa_send[mine, :]
    send_dp(7, lambda peer: pa_send.at[piece(peer)], pa_recv.at[d], pa_recv.at[pl.ds(0, DP - 1)])

    wait_all(6)
    wait_all(7)
    total = e2_recv[0].astype(F32)
    for k in range(1, 4):
        total += e2_recv[k].astype(F32)
    for k in range(DP):
        total += pa_recv[k].astype(F32)
    pfull[y, c, mine, :] = split(fold(total) * (1.0 / DP))
    send_y(8, lambda peer: pfull.at[y, c, mine], pfull.at[y, c, mine], pfull.at[0, 0, pl.ds(0, 3 * PIECE)])

    pass_on(range(W3, CUTS))
    for owner, h in ((down, 1), (up, 0)):
        for i in range(CUTS):
            arrived(owner, h, i)
        ag(owner, h, 0, sib, None, CUTS)
        take(owner, h * HALF, HALF)

    wait_all(8)
    send_dp(9, lambda peer: pfull.at[:, c, mine], pfull.at[:, c, mine],
            pfull.at[:, 0, pl.ds(0, FEAT - PIECE)], p_recv.at[d])
    started[10] = pfull.at[:, 1 - c]
    remote(10, pfull.at[:, c, mine], pfull.at[:, c, mine], {"tp": sib})

    for owner, h in ((odown, 1), (oup, 0)):
        arrived(owner, h, 0, CUTS)
        take(owner, h * HALF, HALF)

    @pl.loop(1, DP)
    def _(k):
        source = lax.rem(d + DP - k, DP)
        block = pfull.at[:, c, piece(source)]
        pltpu.make_async_copy(block, block, p_recv.at[source]).wait()
        remote(10, block, block, {"tp": sib})

    for i in range(0, CUTS, 2):
        for h in range(2):
            arrived(far, h, i)
            arrived(far, h, i + 1)
            ag(far, h, i, sib, None, 2)
    take(far, 0, TOK)

    wait_all(10)
    copy_p = pltpu.make_async_copy(pfull, p_hbm, out_sem.at[TP])
    copy_p.start()
    right = jnp.zeros((128, COLS), F32)
    gram = jnp.zeros((128, 128), F32)
    for k in range(TP):
        pt[k] = pfull[k // 2, k % 2].T
        right += dot(pt[k], ev[k * FEAT : (k + 1) * FEAT, :])
        gram += dot(pt[k], pfull[k // 2, k % 2])
    def left(owner):
        return dot(pt[owner], at[owner])

    ap = left(t)
    for owner in (sib, down, up, odown, oup, far):
        ap += left(owner)

    for i in range(0, CUTS, 2):
        for h in range(2):
            arrived(ofar, h, i, 2)
    take(ofar, 0, TOK)

    @pl.loop(0, TOK // STEP)
    def _(k):
        r = pl.ds(pl.multiple_of(k * STEP, STEP), STEP)
        res[r, :] = (res[r, :].astype(F32) + proj[r, :] - tch[r, :].astype(F32)).astype(BF16)

    ap += left(ofar)
    ap = ap[0:RANK] + ap[RANK:]
    ap_high = ap.astype(BF16).astype(F32)
    ap_cat = jnp.concatenate([ap_high, ap - ap_high], axis=0).astype(BF16)
    right += dot(ap_cat, res[...]) * (1.0 / 32.0)
    right = right[0:RANK] + right[RANK:]
    for i in range(8):
        for j in range(5):
            r_send[i * 5 + j] = right[8 * i : 8 * i + 8, 128 * j : 128 * j + 128]
    for j in range(40, TILES):
        r_send[j] = jnp.zeros((8, 128), F32)
    PER = TILES // DP
    r_recv[d] = r_send[pl.ds(d * PER, PER)]
    send_dp(11, lambda peer: r_send.at[pl.ds(peer * PER, PER)], r_recv.at[d], r_recv.at[pl.ds(0, DP - 1)])

    def stored(k):
        r = pl.ds(k * 2 * FEAT, 2 * FEAT)
        return pltpu.make_async_copy(ev.at[r], m_hbm.at[r], out_sem.at[k])

    def matrix(k):
        r = pl.ds(k * 2 * FEAT, 2 * FEAT)
        grad = dot(at[pl.ds(2 * k, 2)].reshape(2 * FEAT, TOK), res[...]) * (1.0 / 32.0)
        ev[r, :] = (grad + ev[r, :].astype(F32)).astype(BF16)
        stored(k).start()

    matrix(0)
    linv = inverse_factor(fold(gram[0:RANK] + gram[RANK:]))
    lhigh = linv.astype(BF16).astype(F32)
    lcat = split(linv)
    ltcat = jnp.concatenate([lhigh.T[0:RANK], (linv - lhigh).T[0:RANK]], axis=1).astype(BF16)
    matrix(1)

    wait_all(11)
    total = r_recv[0]
    for k in range(1, DP):
        total += r_recv[k]
    r_full[pl.ds(d * PER, PER)] = total
    send_dp(12, lambda peer: r_full.at[pl.ds(d * PER, PER)], r_full.at[pl.ds(d * PER, PER)],
            r_full.at[pl.ds(0, TILES - PER)])

    matrix(2)
    matrix(3)
    wait_all(12)
    summed = jnp.concatenate(
        [jnp.concatenate([r_full[i * 5 + j] for j in range(5)], axis=1) for i in range(8)], axis=0
    )
    rhigh, rlow = split_rows(summed)
    qt = (dot(lcat, rhigh) + dot(lcat, rlow)) * (1.0 / DP)
    qnext_ref[...] = qt
    rhigh, rlow = split_rows(qt)
    coef = dot(ltcat, rhigh) + dot(ltcat, rlow)
    chigh, clow = split_rows(coef)
    coef_ref[...] = jnp.concatenate([chigh, clow], axis=0)

    for i, like in started.items():
        pltpu.make_async_copy(like, like, x_send.at[i]).wait()
    for copy in sends:
        copy.wait_send()
    copy_p.wait()

    for k in range(4):
        stored(k).wait()


CHUNKS = 8
CHUNK = ROWS // CHUNKS


def write_kernel(m_hbm, p_hbm, coef_ref, qt_ref, out_hbm, qout_ref, m, p, out, m_sem, p_sem, out_sem):
    def load(k):
        r = pl.ds(pl.multiple_of(k * CHUNK, CHUNK), CHUNK)
        return (
            pltpu.make_async_copy(m_hbm.at[r], m.at[r], m_sem.at[k]),
            pltpu.make_async_copy(p_hbm.at[k // 2, lax.rem(k, 2)], p.at[r], p_sem.at[k]),
        )

    def store(k):
        r = pl.ds(pl.multiple_of(k * CHUNK, CHUNK), CHUNK)
        return pltpu.make_async_copy(out.at[r], out_hbm.at[r], out_sem.at[k])

    @pl.loop(0, CHUNKS)
    def _(k):
        for copy in load(k):
            copy.start()

    qout_ref[...] = qt_ref[...]

    @pl.loop(0, CHUNKS)
    def _(k):
        for copy in load(k):
            copy.wait()
        r = pl.ds(pl.multiple_of(k * CHUNK, CHUNK), CHUNK)
        cat = p[r, :]
        approx = dot(jnp.concatenate([cat, cat], axis=1), coef_ref[...])
        out[r, :] = (m[r, :].astype(F32) - approx).astype(BF16)
        store(k).start()

    @pl.loop(0, CHUNKS)
    def _(k):
        store(k).wait()


def per_device(attn_out, residual_in, teacher, out_weight, error_buf, q_start):
    any_space = pl.BlockSpec(memory_space=pl.ANY)
    vmem = pl.BlockSpec(memory_space=pltpu.VMEM)
    V, S = pltpu.VMEM, pltpu.SemaphoreType.DMA
    n_ag = CUTS * 2 * 3 + 2 * 5 + 2
    m, p, coef, qt = pl.pallas_call(
        main_kernel,
        name="gather_and_factors",
        out_shape=(
            jax.ShapeDtypeStruct((ROWS, COLS), BF16),
            jax.ShapeDtypeStruct((4, 2, FEAT, 128), BF16),
            jax.ShapeDtypeStruct((256, COLS), BF16),
            jax.ShapeDtypeStruct((RANK, COLS), F32),
        ),
        in_specs=[any_space] * 5 + [vmem],
        out_specs=(any_space, any_space, vmem, vmem),
        scratch_shapes=[
            V((TP, TOK, FEAT), BF16),
            V((TP, FEAT, TOK), BF16),
            V((TP, FEAT, COLS), BF16),
            V((ROWS, COLS), BF16),
            V((TOK, COLS), BF16),
            V((TOK, COLS), BF16),
            V((TOK, COLS), F32),
            V((TP, PIECE, COLS), BF16),
            V((COLS, 128), BF16),
            V((TOK, 128), F32),
            V((TP, PIECE, 128), BF16),
            V((TP, PIECE, 128), BF16),
            V((FEAT, 128), BF16),
            V((TOK, 128), BF16),
            V((TP, TOKP, 128), BF16),
            V((TOK, 128), BF16),
            V((FEAT, 128), BF16),
            V((DP, PIECE, 128), BF16),
            V((4, 2, FEAT, 128), BF16),
            V((4, FEAT, 128), BF16),
            V((4, FEAT, 128), BF16),
            V((DP, 4, PIECE, 128), BF16),
            V((4, PIECE, 128), BF16),
            V((4, PIECE, 128), BF16),
            V((4, 2, FEAT, 128), BF16),
            V((TP, 128, FEAT), BF16),
            V((TILES, 8, 128), F32),
            V((DP, TILES // DP, 8, 128), F32),
            V((TILES, 8, 128), F32),
            S((6,)),
            S((n_ag,)),
            S((TP, 2, CUTS)),
            S((13,)),
            S((13,)),
            S((DP,)),
            S((TP + 1,)),
        ],
        compiler_params=pltpu.CompilerParams(
            collective_id=0, has_side_effects=True, vmem_limit_bytes=60 * 2**20
        ),
    )(
        attn_out, residual_in, teacher,
        out_weight.reshape(TP, FEAT, COLS),
        error_buf[0], q_start.T,
    )
    error_next, q_next = pl.pallas_call(
        write_kernel,
        name="write_error",
        out_shape=(
            jax.ShapeDtypeStruct((ROWS, COLS), BF16),
            jax.ShapeDtypeStruct((RANK, COLS), F32),
        ),
        in_specs=[any_space, any_space, vmem, vmem],
        out_specs=(any_space, vmem),
        scratch_shapes=[
            V((ROWS, COLS), BF16),
            V((ROWS, 128), BF16),
            V((ROWS, COLS), BF16),
            S((CHUNKS,)),
            S((CHUNKS,)),
            S((CHUNKS,)),
        ],
        compiler_params=pltpu.CompilerParams(vmem_limit_bytes=60 * 2**20),
    )(m, p, coef, qt)
    return error_next[None], q_next.T


def solution(mesh):
    return jax.shard_map(
        per_device,
        mesh=mesh,
        in_specs=(
            P("dp", "tp"),
            P("dp", "tp"),
            P("dp", "tp"),
            P(None, "tp"),
            P("dp", None, "tp"),
            P("tp", None),
        ),
        out_specs=(P("dp", None, "tp"), P("tp", None)),
        check_vma=False,
    )
```

```python
import jax
import jax.numpy as jnp
from jax import lax
from jax.experimental import pallas as pl
from jax.experimental.pallas import tpu as pltpu
from jax.sharding import PartitionSpec as P

MESH = pl.DeviceIdType.MESH
F32, BF16 = jnp.float32, jnp.bfloat16
DP, TP = 16, 8
TOK, FEAT, COLS, RANK = 1024, 512, 640, 64
ROWS = FEAT * TP
PIECE = FEAT // DP
TOKP = TOK // TP
HALF = TOK // 2
CUTS = 4
GROUP = 4
CUT = HALF // CUTS
TILES = 48
W2, W3 = 2, 1


def dot(a, b):
    return jnp.dot(a, b, preferred_element_type=F32)


def fold(x):
    return x + pltpu.roll(x, RANK, 1)


def split(x):
    lane = lax.broadcasted_iota(jnp.int32, x.shape, 1)
    high = x.astype(BF16).astype(F32)
    return jnp.where(lane < RANK, high, x - high).astype(BF16)


def split_rows(x):
    high = x.astype(BF16).astype(F32)
    low = x - high
    return (
        jnp.concatenate([high, high], axis=0).astype(BF16),
        jnp.concatenate([low, low], axis=0).astype(BF16),
    )


def inverse_factor(gram):
    lane = lax.broadcasted_iota(jnp.int32, (8, 128), 1)
    sub = lax.broadcasted_iota(jnp.int32, (8, 128), 0)
    blocks = []
    for b in range(8):
        eye = jnp.where(lane == sub + (RANK + 8 * b), 1.0, 0.0)
        blocks.append(jnp.where(lane < RANK, gram[8 * b : 8 * b + 8, :], eye))
    for k in range(0, RANK, GROUP):
        home, at = k // 8, k % 8
        span = range(GROUP)
        row = [jnp.broadcast_to(blocks[home][at + i : at + i + 1, :], (8, 128)) for i in span]
        small = [[jnp.broadcast_to(row[i][:, k + j : k + j + 1], (8, 128)) for j in span] for i in span]
        column = {
            b: [jnp.broadcast_to(blocks[b][:, k + j : k + j + 1], (8, 128)) for j in span] for b in range(home, 8)
        }
        for i in span:
            inverse = 1.0 / small[i][i]
            for j in range(i + 1, GROUP):
                factor = small[i][j] * inverse
                row[j] = row[j] - factor * row[i]
                for l in range(i + 1, GROUP):
                    small[j][l] = small[j][l] - factor * small[i][l]
                for b in column:
                    column[b][j] = column[b][j] - factor * column[b][i]
            row[i] = row[i] * inverse
        for b in column:
            for i in span:
                below = column[b][i]
                if b == home:
                    below = jnp.where(sub > at + i, below, 0.0)
                blocks[b] = blocks[b] - below * row[i]
    out = []
    for b in range(8):
        diagonal = jnp.sum(jnp.where(lane == sub + 8 * b, blocks[b], 0.0), axis=1, keepdims=True)
        rows = jnp.where(lane < RANK, 0.0, blocks[b] * lax.rsqrt(diagonal))
        out.append(fold(rows))
    return jnp.concatenate(out, axis=0)


def main_kernel(
    a_hbm, res_hbm, tch_hbm, w_hbm, e_hbm, qt_ref,
    m_ref, p_ref, coef_ref, qnext_ref,
    abuf, at, wv, ev, res, tch, proj, wblk, qcat, xq,
    wq_send, wq_recv, wq_full, dq_send, dq_recv, dq_full,
    pa_send, pa_recv, eq_send, e0_recv, e1_send, e_recv, e2_send, e2_recv, pfull, pt,
    r_send, r_recv, r_full,
    load_sem, ag_send, ag_recv, x_send, x_recv, p_recv, out_sem,
):
    d, t = lax.axis_index("dp"), lax.axis_index("tp")
    y, c = t // 2, lax.rem(t, 2)
    sib = y * 2 + 1 - c
    up = lax.rem(y + 1, 4) * 2 + c
    down = lax.rem(y + 3, 4) * 2 + c
    far = lax.rem(y + 2, 4) * 2 + c
    odown, oup, ofar = (lax.rem(y + k, 4) * 2 + 1 - c for k in (3, 1, 2))

    mine = pl.ds(pl.multiple_of(d * PIECE, PIECE), PIECE)
    load_blk = pltpu.make_async_copy(w_hbm.at[:, mine], wblk, load_sem.at[0])
    load_a = pltpu.make_async_copy(a_hbm, abuf.at[t], load_sem.at[1])
    load_e = pltpu.make_async_copy(e_hbm, ev, load_sem.at[2])
    load_res = pltpu.make_async_copy(res_hbm, res, load_sem.at[3])
    load_tch = pltpu.make_async_copy(tch_hbm, tch, load_sem.at[4])
    load_w = pltpu.make_async_copy(w_hbm, wv, load_sem.at[5])
    for load in (load_blk, load_res, load_tch, load_e, load_a, load_w):
        load.start()

    barrier = pltpu.get_barrier_semaphore()

    @pl.loop(1, TP)
    def _(k):
        pl.semaphore_signal(barrier, inc=1, device_id={"tp": lax.rem(t + k, TP)}, device_id_type=MESH)

    @pl.loop(1, DP)
    def _(k):
        pl.semaphore_signal(barrier, inc=1, device_id={"dp": lax.rem(d + k, DP)}, device_id_type=MESH)

    q = qt_ref[...]
    high = q.astype(BF16).astype(F32)
    qcat[...] = jnp.concatenate([high, q - high], axis=0).T.astype(BF16)

    load_blk.wait()
    part = dot(wblk[...].reshape(TP * PIECE, COLS), qcat[...])
    wq_send[...] = split(fold(part)).reshape(TP, PIECE, 128)
    wq_recv[t] = wq_send[t]

    load_res.wait()
    load_tch.wait()
    STEP = 512

    @pl.loop(0, TOK // STEP)
    def _(k):
        r = pl.ds(pl.multiple_of(k * STEP, STEP), STEP)
        xq[r, :] = dot(res[r, :], qcat[...]) - dot(tch[r, :], qcat[...])

    pl.semaphore_wait(barrier, TP - 1 + DP - 1)

    started = {}

    def remote(i, src, dst, peer, recv=None):
        pltpu.make_async_remote_copy(
            src, dst, x_send.at[i], x_recv.at[i] if recv is None else recv,
            device_id=peer, device_id_type=MESH,
        ).start()

    def send_tp(i, src, dst, like):
        started[i] = like

        @pl.loop(1, TP)
        def _(k):
            peer = lax.rem(t + k, TP)
            remote(i, src(peer), dst, {"tp": peer})

    def send_y(i, src, dst, like):
        started[i] = like

        @pl.loop(1, 4)
        def _(k):
            peer = lax.rem(y + k, 4)
            remote(i, src(peer), dst, {"tp": peer * 2 + c})

    def send_dp(i, src, dst, like, recv=None):
        started[i] = like

        @pl.loop(1, DP)
        def _(k):
            peer = lax.rem(d + k, DP)
            remote(i, src(peer), dst, {"dp": peer}, recv)

    def wait_all(i):
        pltpu.make_async_copy(started[i], started[i], x_recv.at[i]).wait()

    sends = []

    def rows(h, i, n=1):
        return pl.ds(h * HALF + i * CUT, n * CUT)

    def ag(owner, h, i, dest, src=None, n=1):
        r = rows(h, i, n)
        copy = pltpu.make_async_remote_copy(
            abuf.at[owner, r] if src is None else src.at[r], abuf.at[owner, r],
            ag_send.at[len(sends)], ag_recv.at[owner, h, i],
            device_id={"tp": dest}, device_id_type=MESH,
        )
        copy.start()
        sends.append(copy)

    def arrived(owner, h, i, n=1):
        r = rows(h, i, n)
        pltpu.make_async_copy(abuf.at[owner, r], abuf.at[owner, r], ag_recv.at[owner, h, i]).wait()

    def own(hh, pieces):
        for i in pieces:
            ag(t, hh, i, up, a_hbm)
            ag(t, 1 - hh, i, down, a_hbm)

    def pass_on(pieces):
        for i in pieces:
            ag(down, 0, i, up)
            ag(up, 1, i, down)

    send_tp(0, lambda peer: wq_send.at[peer], wq_recv.at[t], wq_recv.at[pl.ds(0, TP - 1)])
    own(0, range(CUTS))

    load_e.wait()

    @pl.loop(0, TP)
    def _(k):
        block = ev[pl.ds(pl.multiple_of(k * FEAT, FEAT), FEAT), :]
        eq_send[k // 2, lax.rem(k, 2)] = split(fold(dot(block, qcat[...])))

    started[1] = e0_recv
    remote(1, eq_send.at[:, 1 - c], e0_recv, {"tp": sib})
    for h in range(2):
        ag(t, h, 0, sib, a_hbm, CUTS)

    def piece(peer):
        return pl.ds(pl.multiple_of(peer * PIECE, PIECE), PIECE)

    wait_all(0)
    total = wq_recv[0].astype(F32)
    for k in range(1, TP):
        total += wq_recv[k].astype(F32)
    wq_full[mine, :] = split(fold(total))
    send_dp(2, lambda peer: wq_full.at[mine], wq_full.at[mine], wq_full.at[pl.ds(0, FEAT - PIECE)])

    wait_all(1)

    @pl.loop(0, 4)
    def _(k):
        e1_send[k] = split(fold(eq_send[k, c].astype(F32) + e0_recv[k].astype(F32)))

    e_recv[d] = e1_send[:, mine, :]
    send_dp(5, lambda peer: e1_send.at[:, piece(peer)], e_recv.at[d], e_recv.at[pl.ds(0, DP - 1)])

    load_a.wait()
    load_w.wait()

    def take(owner, lo, n, first=False):
        @pl.loop(0, n // STEP)
        def _(k):
            r = pl.ds(pl.multiple_of(lo + k * STEP, STEP), STEP)
            block = abuf[owner, r, :]
            at[owner, :, r] = block.T
            term = dot(block, wv[owner])
            if first:
                proj[r, :] = term
            else:
                proj[r, :] += term

    take(t, 0, TOK, first=True)

    wait_all(2)

    @pl.loop(0, TOK // STEP)
    def _(k):
        r = pl.ds(pl.multiple_of(k * STEP, STEP), STEP)
        part = xq[r, :] + dot(abuf[t, r, :], wq_full[...])
        dq_send[r, :] = split(fold(part))

    def tokens(peer):
        return pl.ds(pl.multiple_of(peer * TOKP, TOKP), TOKP)

    dq_recv[t] = dq_send[tokens(t), :]
    send_tp(3, lambda peer: dq_send.at[tokens(peer)], dq_recv.at[t], dq_recv.at[pl.ds(0, TP - 1)])

    own(1, range(0, W2))
    for h in range(2):
        arrived(sib, h, 0, CUTS)
    take(sib, 0, TOK)
    wait_all(3)
    total = dq_recv[0].astype(F32)
    for k in range(1, TP):
        total += dq_recv[k].astype(F32)
    dq_full[tokens(t), :] = split(fold(total))
    send_tp(4, lambda peer: dq_full.at[tokens(t)], dq_full.at[tokens(t)], dq_full.at[pl.ds(0, TOK - TOKP)])

    wait_all(5)

    @pl.loop(0, 4)
    def _(k):
        total = e_recv[0, k].astype(F32)
        for j in range(1, DP):
            total += e_recv[j, k].astype(F32)
        e2_send[k] = split(fold(total))

    e2_recv[y] = e2_send[y]

    send_y(6, lambda peer: e2_send.at[peer], e2_recv.at[y], e2_recv.at[pl.ds(0, 3)])
    own(1, range(W2, CUTS))
    for owner, h in ((down, 0), (up, 1)):
        for i in range(CUTS):
            arrived(owner, h, i)
    pass_on(range(0, W3))
    for owner, h in ((down, 0), (up, 1)):
        ag(owner, h, 0, sib, None, CUTS)
        take(owner, h * HALF, HALF)

    wait_all(4)
    part = dot(at[t], dq_full[...]) * (1.0 / 32.0)
    pa_send[...] = split(fold(part))
    pa_recv[d] = pa_send[mine, :]
    send_dp(7, lambda peer: pa_send.at[piece(peer)], pa_recv.at[d], pa_recv.at[pl.ds(0, DP - 1)])

    for owner, h in ((odown, 0), (oup, 1)):
        arrived(owner, h, 0, CUTS)
        take(owner, h * HALF, HALF)

    wait_all(6)
    wait_all(7)
    total = e2_recv[0].astype(F32)
    for k in range(1, 4):
        total += e2_recv[k].astype(F32)
    for k in range(DP):
        total += pa_recv[k].astype(F32)
    pfull[y, c, mine, :] = split(fold(total) * (1.0 / DP))
    send_y(8, lambda peer: pfull.at[y, c, mine], pfull.at[y, c, mine], pfull.at[0, 0, pl.ds(0, 3 * PIECE)])

    pass_on(range(W3, CUTS))
    for owner, h in ((down, 1), (up, 0)):
        for i in range(CUTS):
            arrived(owner, h, i)
        ag(owner, h, 0, sib, None, CUTS)
        take(owner, h * HALF, HALF)

    wait_all(8)
    send_dp(9, lambda peer: pfull.at[:, c, mine], pfull.at[:, c, mine],
            pfull.at[:, 0, pl.ds(0, FEAT - PIECE)], p_recv.at[d])
    started[10] = pfull.at[:, 1 - c]
    remote(10, pfull.at[:, c, mine], pfull.at[:, c, mine], {"tp": sib})

    for owner, h in ((odown, 1), (oup, 0)):
        arrived(owner, h, 0, CUTS)
        take(owner, h * HALF, HALF)

    def far_pieces(i):
        for h in range(2):
            arrived(far, h, i)
            arrived(far, h, i + 1)
            ag(far, h, i, sib, None, 2)

    far_pieces(0)

    @pl.loop(1, DP)
    def _(k):
        source = lax.rem(d + DP - k, DP)
        block = pfull.at[:, c, piece(source)]
        pltpu.make_async_copy(block, block, p_recv.at[source]).wait()
        remote(10, block, block, {"tp": sib})

    far_pieces(2)
    take(far, 0, TOK)

    wait_all(10)
    copy_p = pltpu.make_async_copy(pfull, p_ref, out_sem)
    copy_p.start()
    right = jnp.zeros((128, COLS), F32)
    for k in range(TP):
        pt[k] = pfull[k // 2, k % 2].T
        right += dot(pt[k], ev[k * FEAT : (k + 1) * FEAT, :])
    def left(owner):
        return dot(pt[owner], at[owner])

    ap = left(t)
    for owner in (sib, down, up, odown, oup, far):
        ap += left(owner)

    for i in range(0, CUTS, 2):
        for h in range(2):
            arrived(ofar, h, i, 2)
    take(ofar, 0, TOK)

    @pl.loop(0, TOK // STEP)
    def _(k):
        r = pl.ds(pl.multiple_of(k * STEP, STEP), STEP)
        res[r, :] = (res[r, :].astype(F32) + proj[r, :] - tch[r, :].astype(F32)).astype(BF16)

    ap += left(ofar)
    ap = ap[0:RANK] + ap[RANK:]
    ap_high = ap.astype(BF16).astype(F32)
    ap_cat = jnp.concatenate([ap_high, ap - ap_high], axis=0).astype(BF16)
    right += dot(ap_cat, res[...]) * (1.0 / 32.0)
    right = right[0:RANK] + right[RANK:]
    for i in range(8):
        for j in range(5):
            r_send[i * 5 + j] = right[8 * i : 8 * i + 8, 128 * j : 128 * j + 128]
    for j in range(40, TILES):
        r_send[j] = jnp.zeros((8, 128), F32)
    PER = TILES // DP
    r_recv[d] = r_send[pl.ds(d * PER, PER)]
    send_dp(11, lambda peer: r_send.at[pl.ds(peer * PER, PER)], r_recv.at[d], r_recv.at[pl.ds(0, DP - 1)])

    def matrix(k):
        r = pl.ds(k * 2 * FEAT, 2 * FEAT)
        grad = dot(at[pl.ds(2 * k, 2)].reshape(2 * FEAT, TOK), res[...]) * (1.0 / 32.0)
        m_ref[r, :] = (grad + ev[r, :].astype(F32)).astype(BF16)

    matrix(0)
    gram = dot(pt[0], pfull[0, 0])
    for k in range(1, TP):
        gram += dot(pt[k], pfull[k // 2, k % 2])
    linv = inverse_factor(fold(gram[0:RANK] + gram[RANK:]))
    lhigh = linv.astype(BF16).astype(F32)
    lcat = split(linv)
    ltcat = jnp.concatenate([lhigh.T[0:RANK], (linv - lhigh).T[0:RANK]], axis=1).astype(BF16)
    matrix(1)

    wait_all(11)
    total = r_recv[0]
    for k in range(1, DP):
        total += r_recv[k]
    r_full[pl.ds(d * PER, PER)] = total
    send_dp(12, lambda peer: r_full.at[pl.ds(d * PER, PER)], r_full.at[pl.ds(d * PER, PER)],
            r_full.at[pl.ds(0, TILES - PER)])

    matrix(2)
    matrix(3)
    wait_all(12)
    summed = jnp.concatenate(
        [jnp.concatenate([r_full[i * 5 + j] for j in range(5)], axis=1) for i in range(8)], axis=0
    )
    rhigh, rlow = split_rows(summed)
    qt = (dot(lcat, rhigh) + dot(lcat, rlow)) * (1.0 / DP)
    qnext_ref[...] = qt
    rhigh, rlow = split_rows(qt)
    coef = dot(ltcat, rhigh) + dot(ltcat, rlow)
    chigh, clow = split_rows(coef)
    coef_ref[...] = jnp.concatenate([chigh, clow], axis=0)

    for i, like in started.items():
        pltpu.make_async_copy(like, like, x_send.at[i]).wait()
    for copy in sends:
        copy.wait_send()
    copy_p.wait()


CHUNKS = 8
CHUNK = ROWS // CHUNKS


def write_kernel(m_ref, p_ref, coef_ref, qt_ref, out_hbm, qout_hbm, out, out_sem):
    def store(k):
        r = pl.ds(pl.multiple_of(k * CHUNK, CHUNK), CHUNK)
        return pltpu.make_async_copy(out.at[r], out_hbm.at[r], out_sem.at[k])

    store_q = pltpu.make_async_copy(qt_ref, qout_hbm, out_sem.at[CHUNKS])
    store_q.start()

    @pl.loop(0, CHUNKS)
    def _(k):
        r = pl.ds(pl.multiple_of(k * CHUNK, CHUNK), CHUNK)
        cat = p_ref[k // 2, lax.rem(k, 2)]
        approx = dot(jnp.concatenate([cat, cat], axis=1), coef_ref[...])
        out[r, :] = (m_ref[r, :].astype(F32) - approx).astype(BF16)
        store(k).start()

    @pl.loop(0, CHUNKS)
    def _(k):
        store(k).wait()

    store_q.wait()


def per_device(attn_out, residual_in, teacher, out_weight, error_buf, q_start):
    any_space = pl.BlockSpec(memory_space=pl.ANY)
    vmem = pl.BlockSpec(memory_space=pltpu.VMEM)
    V, S = pltpu.VMEM, pltpu.SemaphoreType.DMA
    n_ag = CUTS * 2 * 3 + 2 * 5 + 2
    m, p, coef, qt = pl.pallas_call(
        main_kernel,
        name="gather_and_factors",
        out_shape=(
            V((ROWS, COLS), BF16),
            V((4, 2, FEAT, 128), BF16),
            V((256, COLS), BF16),
            V((RANK, COLS), F32),
        ),
        in_specs=[any_space] * 5 + [vmem],
        out_specs=(vmem, vmem, vmem, vmem),
        scratch_shapes=[
            V((TP, TOK, FEAT), BF16),
            V((TP, FEAT, TOK), BF16),
            V((TP, FEAT, COLS), BF16),
            V((ROWS, COLS), BF16),
            V((TOK, COLS), BF16),
            V((TOK, COLS), BF16),
            V((TOK, COLS), F32),
            V((TP, PIECE, COLS), BF16),
            V((COLS, 128), BF16),
            V((TOK, 128), F32),
            V((TP, PIECE, 128), BF16),
            V((TP, PIECE, 128), BF16),
            V((FEAT, 128), BF16),
            V((TOK, 128), BF16),
            V((TP, TOKP, 128), BF16),
            V((TOK, 128), BF16),
            V((FEAT, 128), BF16),
            V((DP, PIECE, 128), BF16),
            V((4, 2, FEAT, 128), BF16),
            V((4, FEAT, 128), BF16),
            V((4, FEAT, 128), BF16),
            V((DP, 4, PIECE, 128), BF16),
            V((4, PIECE, 128), BF16),
            V((4, PIECE, 128), BF16),
            V((4, 2, FEAT, 128), BF16),
            V((TP, 128, FEAT), BF16),
            V((TILES, 8, 128), F32),
            V((DP, TILES // DP, 8, 128), F32),
            V((TILES, 8, 128), F32),
            S((6,)),
            S((n_ag,)),
            S((TP, 2, CUTS)),
            S((13,)),
            S((13,)),
            S((DP,)),
            S,
        ],
        compiler_params=pltpu.CompilerParams(
            collective_id=0, has_side_effects=True, vmem_limit_bytes=50 * 2**20
        ),
    )(
        attn_out, residual_in, teacher,
        out_weight.reshape(TP, FEAT, COLS),
        error_buf[0], q_start.T,
    )
    error_next, q_next = pl.pallas_call(
        write_kernel,
        name="write_error",
        out_shape=(
            jax.ShapeDtypeStruct((ROWS, COLS), BF16),
            jax.ShapeDtypeStruct((RANK, COLS), F32),
        ),
        in_specs=[vmem] * 4,
        out_specs=(any_space, any_space),
        scratch_shapes=[
            V((ROWS, COLS), BF16),
            S((CHUNKS + 1,)),
        ],
        compiler_params=pltpu.CompilerParams(vmem_limit_bytes=16 * 2**20),
    )(m, p, coef, qt)
    return error_next[None], q_next.T


def solution(mesh):
    return jax.shard_map(
        per_device,
        mesh=mesh,
        in_specs=(
            P("dp", "tp"),
            P("dp", "tp"),
            P("dp", "tp"),
            P(None, "tp"),
            P("dp", None, "tp"),
            P("tp", None),
        ),
        out_specs=(P("dp", None, "tp"), P("tp", None)),
        check_vma=False,
    )
```

```python
import jax
import jax.numpy as jnp
from jax import lax
from jax.experimental import pallas as pl
from jax.experimental.pallas import tpu as pltpu
from jax.sharding import PartitionSpec as P

MESH = pl.DeviceIdType.MESH
F32, BF16 = jnp.float32, jnp.bfloat16
DP, TP = 16, 8
TOK, FEAT, COLS, RANK = 1024, 512, 640, 64
ROWS = FEAT * TP
PIECE = FEAT // DP
TOKP = TOK // TP
HALF = TOK // 2
CUTS = 4
GROUP = 4
CUT = HALF // CUTS
TILES = 48
W2, W3 = 2, 1


def dot(a, b):
    return jnp.dot(a, b, preferred_element_type=F32)


def fold(x):
    return x + pltpu.roll(x, RANK, 1)


def split(x):
    lane = lax.broadcasted_iota(jnp.int32, x.shape, 1)
    high = x.astype(BF16).astype(F32)
    return jnp.where(lane < RANK, high, x - high).astype(BF16)


def split_rows(x):
    high = x.astype(BF16).astype(F32)
    low = x - high
    return (
        jnp.concatenate([high, high], axis=0).astype(BF16),
        jnp.concatenate([low, low], axis=0).astype(BF16),
    )


def inverse_factor(gram):
    lane = lax.broadcasted_iota(jnp.int32, (8, 128), 1)
    sub = lax.broadcasted_iota(jnp.int32, (8, 128), 0)
    blocks = []
    for b in range(8):
        eye = jnp.where(lane == sub + (RANK + 8 * b), 1.0, 0.0)
        blocks.append(jnp.where(lane < RANK, gram[8 * b : 8 * b + 8, :], eye))
    for k in range(0, RANK, GROUP):
        home, at = k // 8, k % 8
        span = range(GROUP)
        row = [jnp.broadcast_to(blocks[home][at + i : at + i + 1, :], (8, 128)) for i in span]
        small = [[jnp.broadcast_to(row[i][:, k + j : k + j + 1], (8, 128)) for j in span] for i in span]
        column = {
            b: [jnp.broadcast_to(blocks[b][:, k + j : k + j + 1], (8, 128)) for j in span] for b in range(home, 8)
        }
        for i in span:
            inverse = 1.0 / small[i][i]
            for j in range(i + 1, GROUP):
                factor = small[i][j] * inverse
                row[j] = row[j] - factor * row[i]
                for l in range(i + 1, GROUP):
                    small[j][l] = small[j][l] - factor * small[i][l]
                for b in column:
                    column[b][j] = column[b][j] - factor * column[b][i]
            row[i] = row[i] * inverse
        for b in column:
            for i in span:
                below = column[b][i]
                if b == home:
                    below = jnp.where(sub > at + i, below, 0.0)
                blocks[b] = blocks[b] - below * row[i]
    out = []
    for b in range(8):
        diagonal = jnp.sum(jnp.where(lane == sub + 8 * b, blocks[b], 0.0), axis=1, keepdims=True)
        rows = jnp.where(lane < RANK, 0.0, blocks[b] * lax.rsqrt(diagonal))
        out.append(fold(rows))
    return jnp.concatenate(out, axis=0)


def main_kernel(
    a_hbm, res_hbm, tch_hbm, w_hbm, e_hbm, qt_ref,
    m_ref, p_ref, coef_ref, qnext_ref,
    abuf, at, wv, ev, res, tch, proj, wblk, qcat, xq,
    wq_send, wq_recv, wq_full, dq_send, dq_recv, dq_full,
    pa_send, pa_recv, eq_send, e0_recv, e1_send, e_recv, e2_send, e2_recv, pfull, pt,
    r_send, r_recv, r_full,
    load_sem, ag_send, ag_recv, x_send, x_recv, p_recv, out_sem,
):
    d, t = lax.axis_index("dp"), lax.axis_index("tp")
    y, c = t // 2, lax.rem(t, 2)
    sib = y * 2 + 1 - c
    up = lax.rem(y + 1, 4) * 2 + c
    down = lax.rem(y + 3, 4) * 2 + c
    far = lax.rem(y + 2, 4) * 2 + c
    odown, oup, ofar = (lax.rem(y + k, 4) * 2 + 1 - c for k in (3, 1, 2))

    mine = pl.ds(pl.multiple_of(d * PIECE, PIECE), PIECE)
    load_blk = pltpu.make_async_copy(w_hbm.at[:, mine], wblk, load_sem.at[0])
    load_a = pltpu.make_async_copy(a_hbm, abuf.at[t], load_sem.at[1])
    load_e = pltpu.make_async_copy(e_hbm, ev, load_sem.at[2])
    load_res = pltpu.make_async_copy(res_hbm, res, load_sem.at[3])
    load_tch = pltpu.make_async_copy(tch_hbm, tch, load_sem.at[4])
    load_w = pltpu.make_async_copy(w_hbm, wv, load_sem.at[5])
    for load in (load_blk, load_e, load_a, load_res, load_tch, load_w):
        load.start()

    STEP = 512
    barrier = pltpu.get_barrier_semaphore()

    @pl.loop(1, TP)
    def _(k):
        pl.semaphore_signal(barrier, inc=1, device_id={"tp": lax.rem(t + k, TP)}, device_id_type=MESH)

    @pl.loop(1, DP)
    def _(k):
        pl.semaphore_signal(barrier, inc=1, device_id={"dp": lax.rem(d + k, DP)}, device_id_type=MESH)

    q = qt_ref[...]
    high = q.astype(BF16).astype(F32)
    qcat[...] = jnp.concatenate([high, q - high], axis=0).T.astype(BF16)

    load_blk.wait()
    part = dot(wblk[...].reshape(TP * PIECE, COLS), qcat[...])
    wq_send[...] = split(fold(part)).reshape(TP, PIECE, 128)
    wq_recv[t] = wq_send[t]

    pl.semaphore_wait(barrier, TP - 1 + DP - 1)

    started = {}

    def remote(i, src, dst, peer, recv=None):
        pltpu.make_async_remote_copy(
            src, dst, x_send.at[i], x_recv.at[i] if recv is None else recv,
            device_id=peer, device_id_type=MESH,
        ).start()

    def send_tp(i, src, dst, like):
        started[i] = like

        @pl.loop(1, TP)
        def _(k):
            peer = lax.rem(t + k, TP)
            remote(i, src(peer), dst, {"tp": peer})

    def send_y(i, src, dst, like):
        started[i] = like

        @pl.loop(1, 4)
        def _(k):
            peer = lax.rem(y + k, 4)
            remote(i, src(peer), dst, {"tp": peer * 2 + c})

    def send_dp(i, src, dst, like, recv=None):
        started[i] = like

        @pl.loop(1, DP)
        def _(k):
            peer = lax.rem(d + k, DP)
            remote(i, src(peer), dst, {"dp": peer}, recv)

    def wait_all(i):
        pltpu.make_async_copy(started[i], started[i], x_recv.at[i]).wait()

    sends = []

    def rows(h, i, n=1):
        return pl.ds(h * HALF + i * CUT, n * CUT)

    def ag(owner, h, i, dest, src=None, n=1):
        r = rows(h, i, n)
        copy = pltpu.make_async_remote_copy(
            abuf.at[owner, r] if src is None else src.at[r], abuf.at[owner, r],
            ag_send.at[len(sends)], ag_recv.at[owner, h, i],
            device_id={"tp": dest}, device_id_type=MESH,
        )
        copy.start()
        sends.append(copy)

    def arrived(owner, h, i, n=1):
        r = rows(h, i, n)
        pltpu.make_async_copy(abuf.at[owner, r], abuf.at[owner, r], ag_recv.at[owner, h, i]).wait()

    def own(hh, pieces):
        for i in pieces:
            ag(t, hh, i, up, a_hbm)
            ag(t, 1 - hh, i, down, a_hbm)

    def pass_on(pieces):
        for i in pieces:
            ag(down, 0, i, up)
            ag(up, 1, i, down)

    send_tp(0, lambda peer: wq_send.at[peer], wq_recv.at[t], wq_recv.at[pl.ds(0, TP - 1)])
    own(0, range(CUTS))

    load_e.wait()

    @pl.loop(0, TP)
    def _(k):
        block = ev[pl.ds(pl.multiple_of(k * FEAT, FEAT), FEAT), :]
        eq_send[k // 2, lax.rem(k, 2)] = split(fold(dot(block, qcat[...])))

    started[1] = e0_recv
    remote(1, eq_send.at[:, 1 - c], e0_recv, {"tp": sib})
    for h in range(2):
        ag(t, h, 0, sib, a_hbm, CUTS)

    def piece(peer):
        return pl.ds(pl.multiple_of(peer * PIECE, PIECE), PIECE)

    wait_all(0)
    total = wq_recv[0].astype(F32)
    for k in range(1, TP):
        total += wq_recv[k].astype(F32)
    wq_full[mine, :] = split(fold(total))
    send_dp(2, lambda peer: wq_full.at[mine], wq_full.at[mine], wq_full.at[pl.ds(0, FEAT - PIECE)])

    wait_all(1)

    @pl.loop(0, 4)
    def _(k):
        e1_send[k] = split(fold(eq_send[k, c].astype(F32) + e0_recv[k].astype(F32)))

    e_recv[d] = e1_send[:, mine, :]
    send_dp(5, lambda peer: e1_send.at[:, piece(peer)], e_recv.at[d], e_recv.at[pl.ds(0, DP - 1)])

    load_res.wait()
    load_tch.wait()

    @pl.loop(0, TOK // STEP)
    def _(k):
        r = pl.ds(pl.multiple_of(k * STEP, STEP), STEP)
        xq[r, :] = dot(res[r, :], qcat[...]) - dot(tch[r, :], qcat[...])

    load_a.wait()
    load_w.wait()

    def take(owner, lo, n, first=False):
        @pl.loop(0, n // STEP)
        def _(k):
            r = pl.ds(pl.multiple_of(lo + k * STEP, STEP), STEP)
            block = abuf[owner, r, :]
            at[owner, :, r] = block.T
            term = dot(block, wv[owner])
            if first:
                proj[r, :] = term
            else:
                proj[r, :] += term

    take(t, 0, TOK, first=True)

    wait_all(2)

    @pl.loop(0, TOK // STEP)
    def _(k):
        r = pl.ds(pl.multiple_of(k * STEP, STEP), STEP)
        part = xq[r, :] + dot(abuf[t, r, :], wq_full[...])
        dq_send[r, :] = split(fold(part))

    def tokens(peer):
        return pl.ds(pl.multiple_of(peer * TOKP, TOKP), TOKP)

    dq_recv[t] = dq_send[tokens(t), :]
    send_tp(3, lambda peer: dq_send.at[tokens(peer)], dq_recv.at[t], dq_recv.at[pl.ds(0, TP - 1)])

    own(1, range(0, W2))
    for h in range(2):
        arrived(sib, h, 0, CUTS)
    take(sib, 0, TOK)
    wait_all(3)
    total = dq_recv[0].astype(F32)
    for k in range(1, TP):
        total += dq_recv[k].astype(F32)
    dq_full[tokens(t), :] = split(fold(total))
    send_tp(4, lambda peer: dq_full.at[tokens(t)], dq_full.at[tokens(t)], dq_full.at[pl.ds(0, TOK - TOKP)])

    wait_all(5)

    @pl.loop(0, 4)
    def _(k):
        total = e_recv[0, k].astype(F32)
        for j in range(1, DP):
            total += e_recv[j, k].astype(F32)
        e2_send[k] = split(fold(total))

    e2_recv[y] = e2_send[y]

    send_y(6, lambda peer: e2_send.at[peer], e2_recv.at[y], e2_recv.at[pl.ds(0, 3)])
    own(1, range(W2, CUTS))
    for owner, h in ((down, 0), (up, 1)):
        for i in range(CUTS):
            arrived(owner, h, i)
    pass_on(range(0, W3))
    for owner, h in ((down, 0), (up, 1)):
        ag(owner, h, 0, sib, None, CUTS)
        take(owner, h * HALF, HALF)

    wait_all(4)
    part = dot(at[t], dq_full[...]) * (1.0 / 32.0)
    pa_send[...] = split(fold(part))
    pa_recv[d] = pa_send[mine, :]
    send_dp(7, lambda peer: pa_send.at[piece(peer)], pa_recv.at[d], pa_recv.at[pl.ds(0, DP - 1)])

    for owner, h in ((odown, 0), (oup, 1)):
        arrived(owner, h, 0, CUTS)
        take(owner, h * HALF, HALF)

    wait_all(6)
    wait_all(7)
    total = e2_recv[0].astype(F32)
    for k in range(1, 4):
        total += e2_recv[k].astype(F32)
    for k in range(DP):
        total += pa_recv[k].astype(F32)
    pfull[y, c, mine, :] = split(fold(total) * (1.0 / DP))
    send_y(8, lambda peer: pfull.at[y, c, mine], pfull.at[y, c, mine], pfull.at[0, 0, pl.ds(0, 3 * PIECE)])

    pass_on(range(W3, CUTS))
    for owner, h in ((down, 1), (up, 0)):
        for i in range(CUTS):
            arrived(owner, h, i)
        ag(owner, h, 0, sib, None, CUTS)
        take(owner, h * HALF, HALF)

    wait_all(8)
    send_dp(9, lambda peer: pfull.at[:, c, mine], pfull.at[:, c, mine],
            pfull.at[:, 0, pl.ds(0, FEAT - PIECE)], p_recv.at[d])
    started[10] = pfull.at[:, 1 - c]
    remote(10, pfull.at[:, c, mine], pfull.at[:, c, mine], {"tp": sib})

    for owner, h in ((odown, 1), (oup, 0)):
        arrived(owner, h, 0, CUTS)
        take(owner, h * HALF, HALF)

    def far_pieces(i):
        for h in range(2):
            arrived(far, h, i)
            arrived(far, h, i + 1)
            ag(far, h, i, sib, None, 2)

    far_pieces(0)

    @pl.loop(1, DP)
    def _(k):
        source = lax.rem(d + DP - k, DP)
        block = pfull.at[:, c, piece(source)]
        pltpu.make_async_copy(block, block, p_recv.at[source]).wait()
        remote(10, block, block, {"tp": sib})

    far_pieces(2)
    take(far, 0, TOK)

    wait_all(10)
    copy_p = pltpu.make_async_copy(pfull, p_ref, out_sem)
    copy_p.start()
    right = jnp.zeros((128, COLS), F32)
    for k in range(TP):
        pt[k] = pfull[k // 2, k % 2].T
        right += dot(pt[k], ev[k * FEAT : (k + 1) * FEAT, :])
    def left(owner):
        return dot(pt[owner], at[owner])

    ap = left(t)
    for owner in (sib, down, up, odown, oup, far):
        ap += left(owner)

    for i in range(0, CUTS, 2):
        for h in range(2):
            arrived(ofar, h, i, 2)
    take(ofar, 0, TOK)

    @pl.loop(0, TOK // STEP)
    def _(k):
        r = pl.ds(pl.multiple_of(k * STEP, STEP), STEP)
        res[r, :] = (res[r, :].astype(F32) + proj[r, :] - tch[r, :].astype(F32)).astype(BF16)

    ap += left(ofar)
    ap = ap[0:RANK] + ap[RANK:]
    ap_high = ap.astype(BF16).astype(F32)
    ap_cat = jnp.concatenate([ap_high, ap - ap_high], axis=0).astype(BF16)
    right += dot(ap_cat, res[...]) * (1.0 / 32.0)
    right = right[0:RANK] + right[RANK:]
    for i in range(8):
        for j in range(5):
            r_send[i * 5 + j] = right[8 * i : 8 * i + 8, 128 * j : 128 * j + 128]
    for j in range(40, TILES):
        r_send[j] = jnp.zeros((8, 128), F32)
    PER = TILES // DP
    r_recv[d] = r_send[pl.ds(d * PER, PER)]
    send_dp(11, lambda peer: r_send.at[pl.ds(peer * PER, PER)], r_recv.at[d], r_recv.at[pl.ds(0, DP - 1)])

    def matrix(k):
        r = pl.ds(k * 2 * FEAT, 2 * FEAT)
        grad = dot(at[pl.ds(2 * k, 2)].reshape(2 * FEAT, TOK), res[...]) * (1.0 / 32.0)
        m_ref[r, :] = (grad + ev[r, :].astype(F32)).astype(BF16)

    matrix(0)
    gram = dot(pt[0], pfull[0, 0])
    for k in range(1, TP):
        gram += dot(pt[k], pfull[k // 2, k % 2])
    linv = inverse_factor(fold(gram[0:RANK] + gram[RANK:]))
    lhigh = linv.astype(BF16).astype(F32)
    lcat = split(linv)
    ltcat = jnp.concatenate([lhigh.T[0:RANK], (linv - lhigh).T[0:RANK]], axis=1).astype(BF16)
    matrix(1)

    wait_all(11)
    total = r_recv[0]
    for k in range(1, DP):
        total += r_recv[k]
    r_full[pl.ds(d * PER, PER)] = total
    send_dp(12, lambda peer: r_full.at[pl.ds(d * PER, PER)], r_full.at[pl.ds(d * PER, PER)],
            r_full.at[pl.ds(0, TILES - PER)])

    matrix(2)
    matrix(3)
    wait_all(12)
    summed = jnp.concatenate(
        [jnp.concatenate([r_full[i * 5 + j] for j in range(5)], axis=1) for i in range(8)], axis=0
    )
    rhigh, rlow = split_rows(summed)
    qt = (dot(lcat, rhigh) + dot(lcat, rlow)) * (1.0 / DP)
    qnext_ref[...] = qt
    rhigh, rlow = split_rows(qt)
    coef = dot(ltcat, rhigh) + dot(ltcat, rlow)
    chigh, clow = split_rows(coef)
    coef_ref[...] = jnp.concatenate([chigh, clow], axis=0)

    for i, like in started.items():
        pltpu.make_async_copy(like, like, x_send.at[i]).wait()
    for copy in sends:
        copy.wait_send()
    copy_p.wait()


CHUNKS = 8
CHUNK = ROWS // CHUNKS


def write_kernel(m_ref, p_ref, coef_ref, qt_ref, out_hbm, qout_hbm, out, out_sem):
    def store(k):
        r = pl.ds(pl.multiple_of(k * CHUNK, CHUNK), CHUNK)
        return pltpu.make_async_copy(out.at[r], out_hbm.at[r], out_sem.at[k])

    store_q = pltpu.make_async_copy(qt_ref, qout_hbm, out_sem.at[CHUNKS])
    store_q.start()

    @pl.loop(0, CHUNKS)
    def _(k):
        r = pl.ds(pl.multiple_of(k * CHUNK, CHUNK), CHUNK)
        cat = p_ref[k // 2, lax.rem(k, 2)]
        approx = dot(jnp.concatenate([cat, cat], axis=1), coef_ref[...])
        out[r, :] = (m_ref[r, :].astype(F32) - approx).astype(BF16)
        store(k).start()

    @pl.loop(0, CHUNKS)
    def _(k):
        store(k).wait()

    store_q.wait()


def per_device(attn_out, residual_in, teacher, out_weight, error_buf, q_start):
    any_space = pl.BlockSpec(memory_space=pl.ANY)
    vmem = pl.BlockSpec(memory_space=pltpu.VMEM)
    V, S = pltpu.VMEM, pltpu.SemaphoreType.DMA
    n_ag = CUTS * 2 * 3 + 2 * 5 + 2
    m, p, coef, qt = pl.pallas_call(
        main_kernel,
        name="gather_and_factors",
        out_shape=(
            V((ROWS, COLS), BF16),
            V((4, 2, FEAT, 128), BF16),
            V((256, COLS), BF16),
            V((RANK, COLS), F32),
        ),
        in_specs=[any_space] * 5 + [vmem],
        out_specs=(vmem, vmem, vmem, vmem),
        scratch_shapes=[
            V((TP, TOK, FEAT), BF16),
            V((TP, FEAT, TOK), BF16),
            V((TP, FEAT, COLS), BF16),
            V((ROWS, COLS), BF16),
            V((TOK, COLS), BF16),
            V((TOK, COLS), BF16),
            V((TOK, COLS), F32),
            V((TP, PIECE, COLS), BF16),
            V((COLS, 128), BF16),
            V((TOK, 128), F32),
            V((TP, PIECE, 128), BF16),
            V((TP, PIECE, 128), BF16),
            V((FEAT, 128), BF16),
            V((TOK, 128), BF16),
            V((TP, TOKP, 128), BF16),
            V((TOK, 128), BF16),
            V((FEAT, 128), BF16),
            V((DP, PIECE, 128), BF16),
            V((4, 2, FEAT, 128), BF16),
            V((4, FEAT, 128), BF16),
            V((4, FEAT, 128), BF16),
            V((DP, 4, PIECE, 128), BF16),
            V((4, PIECE, 128), BF16),
            V((4, PIECE, 128), BF16),
            V((4, 2, FEAT, 128), BF16),
            V((TP, 128, FEAT), BF16),
            V((TILES, 8, 128), F32),
            V((DP, TILES // DP, 8, 128), F32),
            V((TILES, 8, 128), F32),
            S((6,)),
            S((n_ag,)),
            S((TP, 2, CUTS)),
            S((13,)),
            S((13,)),
            S((DP,)),
            S,
        ],
        compiler_params=pltpu.CompilerParams(
            collective_id=0, has_side_effects=True, vmem_limit_bytes=50 * 2**20
        ),
    )(
        attn_out, residual_in, teacher,
        out_weight.reshape(TP, FEAT, COLS),
        error_buf[0], q_start.T,
    )
    error_next, q_next = pl.pallas_call(
        write_kernel,
        name="write_error",
        out_shape=(
            jax.ShapeDtypeStruct((ROWS, COLS), BF16),
            jax.ShapeDtypeStruct((RANK, COLS), F32),
        ),
        in_specs=[vmem] * 4,
        out_specs=(any_space, any_space),
        scratch_shapes=[
            V((ROWS, COLS), BF16),
            S((CHUNKS + 1,)),
        ],
        compiler_params=pltpu.CompilerParams(vmem_limit_bytes=16 * 2**20),
    )(m, p, coef, qt)
    return error_next[None], q_next.T


def solution(mesh):
    return jax.shard_map(
        per_device,
        mesh=mesh,
        in_specs=(
            P("dp", "tp"),
            P("dp", "tp"),
            P("dp", "tp"),
            P(None, "tp"),
            P("dp", None, "tp"),
            P("tp", None),
        ),
        out_specs=(P("dp", None, "tp"), P("tp", None)),
        check_vma=False,
    )
```
